32 devices in a mesh: grp: 2 (over y), batch: 16 (over z, x, core).
Axes of the slice: x: 2, y: 2, z: 4, core: 2. Of those that a mesh axis runs over, the one named last changes fastest.
Arguments:
- tokens: bfloat16 [32768, 768], P(('grp', 'batch')), may hold values from -6 to 6
- buckets: int32 [64], P(('grp', 'batch')), may hold values from 0 to 2, as said below
- lengths: int32 [64, 16], P(('grp', 'batch')), may hold values from 0 to 256, as said below
- positives: int32 [512], replicated, may hold values from 0 to 95
- w_query: bfloat16 [768, 768], replicated, may hold values from -0.21875 to 0.21875
- b_query: float32 [768], replicated, may hold values from -3 to 3
- w_key: bfloat16 [768, 768], replicated, may hold values from -0.21875 to 0.21875
- w_value: bfloat16 [768, 768], replicated, may hold values from -0.21875 to 0.21875
- b_value: float32 [768], replicated, may hold values from -3 to 3
- w_out: bfloat16 [768, 768], replicated, may hold values from -1.25 to 1.25
- b_out: float32 [768], replicated, may hold values from -3 to 3
- gain_attn: float32 [768], replicated, may hold values from 0.25 to 1.75
- shift_attn: float32 [768], replicated, may hold values from -1.2 to 1.2
- w_in: bfloat16 [768, 3072], replicated, may hold values from -0.21875 to 0.21875
- b_in: float32 [3072], replicated, may hold values from -3 to 3
- w_back: bfloat16 [3072, 768], replicated, may hold values from -0.109375 to 0.109375
- b_back: float32 [768], replicated, may hold values from -3 to 3
- gain_ffn: float32 [768], replicated, may hold values from 0.25 to 1.75
- shift_ffn: float32 [768], replicated, may hold values from -1.2 to 1.2
Outputs:
- encoded: bfloat16 [32768, 768], P(('grp', 'batch'))
- grad_tokens: float32 [32768, 768], P(('grp', 'batch'))
- grad_w_query: float32 [768, 768], P('batch')
- grad_b_query: float32 [768], P('batch')
- grad_w_key: float32 [768, 768], P('batch')
- grad_w_value: float32 [768, 768], P('batch')
- grad_b_value: float32 [768], P('batch')
- grad_w_out: float32 [768, 768], P('batch')
- grad_b_out: float32 [768], P('batch')
- grad_gain_attn: float32 [768], P('batch')
- grad_shift_attn: float32 [768], P('batch')
- grad_w_in: float32 [768, 3072], P('batch')
- grad_b_in: float32 [3072], P('batch')
- grad_w_back: float32 [3072, 768], P('batch')
- grad_b_back: float32 [768], P('batch')
- grad_gain_ffn: float32 [768], P('batch')
- grad_shift_ffn: float32 [768], P('batch')
The draws below stay inside these ranges and needn't reach their ends.
Inputs may be any that keep to these rules, and one draw needn't show every extreme that they name: `buckets`: blocks of the devices of grp index 0 are 0. On every other device the blocks come in pairs (blocks 0 and 1, 2 and 3, ...) holding one 1 and one 2. lengths[b, s] is 0 where s times the slot size of block b is 512 or more, and otherwise 1 to that slot size; in every block one slot is full.
All inputs are finite; a program needn't handle non-finite values.
Results may differ from the reference program's by a relative error of at most 0.014.
Values may be sent and summed in bfloat16 or wider, within the bound.
A program may use at most 192 MiB of HBM per device.

```python
import jax
import jax.numpy as jnp
from jax import lax

D = 768
H = 12
HD = 64
FF = 3072
QLEN = 32
SHORT = 128
LONG = 256
BLK = 512
SLOTS_BLK = 16
BLK_DEV = 2
TOK_DEV = 1024
PAS_DEV = 6
NBLOCKS = 64
TOKENS = 32768
QUERIES = 512
PASSAGES = 96
N_BATCH = 16
DEVICES = 32


def bucket_table(key):
    flips = jax.random.randint(key, (NBLOCKS // 2,), 0, 2).astype(jnp.int32)
    paired = jnp.stack([1 + flips, 2 - flips], axis=1).reshape(-1)
    block_index = jnp.arange(NBLOCKS, dtype=jnp.int32)
    group_index = block_index // (BLK_DEV * N_BATCH)
    return jnp.where(group_index == 0, 0, paired).astype(jnp.int32)


def draw_buckets(key, part):
    return bucket_table(key)


def draw_lengths(key, part):
    bucket_ids = bucket_table(key)
    key = jax.random.fold_in(key, 7)
    key_lengths, key_full = jax.random.split(key)
    slot_size = jnp.where(bucket_ids == 0, QLEN, jnp.where(bucket_ids == 1, SHORT, LONG)).astype(jnp.int32)
    slot_count = BLK // slot_size
    slot_index = jnp.arange(SLOTS_BLK, dtype=jnp.int32)[None, :]
    drawn = jax.random.randint(key_lengths, (NBLOCKS, SLOTS_BLK), 1, slot_size[:, None] + 1).astype(jnp.int32)
    full_slot = jax.random.randint(key_full, (NBLOCKS,), 0, slot_count).astype(jnp.int32)
    filled = jnp.where(slot_index == full_slot[:, None], slot_size[:, None], drawn)
    return jnp.where(slot_index < slot_count[:, None], filled, 0).astype(jnp.int32)


def with_ends(array, rng, low, largest):
    longest = array.shape.index(max(array.shape))
    spots = []
    for shift in (0, 1):
        where = [jax.random.randint(jax.random.fold_in(rng, axis), (), 0, length) for axis, length in enumerate(array.shape)]
        where[longest] = (where[longest] + shift) % array.shape[longest]
        spots.append(tuple(where))
    return array.at[spots[0]].set(low).at[spots[1]].set(largest)


def shard_levels(stream_key, extent, cuts, least, largest):
    factor_of = 1.0
    for position, blocks in cuts:
        steps = jax.random.uniform(jax.random.fold_in(jax.random.fold_in(stream_key, 6), position), (blocks,), jnp.float32, least / len(cuts), largest / len(cuts))
        factor_of = factor_of * jnp.repeat(jnp.exp(steps), extent[position] // blocks).reshape((-1,) + (1,) * (len(extent) - 1 - position))
    return factor_of


def centred(key, dims, scale, reach, cuts=(), kind=jnp.bfloat16):
    values = scale * jax.random.normal(key, dims, jnp.float32)
    if cuts:
        values = values * shard_levels(key, dims, cuts, -0.22, 0.18)
    return jnp.clip(values, -reach, reach).astype(kind)


def setup_inputs(seed: int = 0) -> dict:
    seeds = jax.random.split(jax.random.key(seed), 20)
    return {
        "tokens": centred(seeds[0], (TOKENS, D), 1.0, 6.0, ((0, 32),)),
        "buckets": draw_buckets(jax.random.fold_in(seeds[19], 71), 0),
        "lengths": draw_lengths(jax.random.fold_in(seeds[19], 71), 0),
        "positives": with_ends(jax.random.randint(seeds[3], (QUERIES,), 0, PASSAGES), jax.random.fold_in(seeds[3], 1), 0, PASSAGES - 1).astype(jnp.int32),
        "w_query": centred(seeds[4], (D, D), D ** -0.5, 0.21875),
        "b_query": centred(seeds[5], (D,), 0.5, 3.0, (), jnp.float32),
        "w_key": centred(seeds[6], (D, D), D ** -0.5, 0.21875),
        "w_value": centred(seeds[7], (D, D), D ** -0.5, 0.21875),
        "b_value": centred(seeds[8], (D,), 0.5, 3.0, (), jnp.float32),
        "w_out": centred(seeds[9], (D, D), (D // 32) ** -0.5, 1.25),
        "b_out": centred(seeds[10], (D,), 0.5, 3.0, (), jnp.float32),
        "gain_attn": jnp.clip(1.0 + 0.15 * jax.random.normal(seeds[11], (D,), jnp.float32), 0.25, 1.75),
        "shift_attn": centred(seeds[12], (D,), 0.2, 1.2, (), jnp.float32),
        "w_in": centred(seeds[13], (D, FF), D ** -0.5, 0.21875),
        "b_in": centred(seeds[14], (FF,), 0.5, 3.0, (), jnp.float32),
        "w_back": centred(seeds[15], (FF, D), FF ** -0.5, 0.109375),
        "b_back": centred(seeds[16], (D,), 0.5, 3.0, (), jnp.float32),
        "gain_ffn": jnp.clip(1.0 + 0.15 * jax.random.normal(seeds[17], (D,), jnp.float32), 0.25, 1.75),
        "shift_ffn": centred(seeds[18], (D,), 0.2, 1.2, (), jnp.float32),
    }


@jax.custom_vjp
def low(v):
    return lax.optimization_barrier(v.astype(jnp.bfloat16)).astype(jnp.float32)

@jax.custom_vjp
def low_back(v):
    return v

def low_keep(v):
    return (low(v), None)

def low_pass(kept, grad):
    return (grad,)

def back_keep(v):
    return (v, None)

def back_low(kept, grad):
    return (low(grad),)
low.defvjp(low_keep, low_pass)
low_back.defvjp(back_keep, back_low)
norm_epsilon = 1e-06

def matmul(left, right):
    return jnp.dot(left, right, precision=lax.Precision.HIGHEST, preferred_element_type=jnp.float32)

def slot_sizes(buckets):
    return jnp.where(buckets == 0, QLEN, jnp.where(buckets == 1, SHORT, LONG)).astype(jnp.int32)

def candidates(buckets):
    sizes_here = slot_sizes(buckets)
    slot_index = jnp.arange(SLOTS_BLK, dtype=jnp.int32)
    starts = slot_index[None, :] * sizes_here[:, None]
    inside = starts < BLK
    return (jnp.where(inside, starts, 0).astype(jnp.int32), inside)

def compact_order(inside):
    flattened = inside.reshape(-1)
    places = jnp.arange(flattened.shape[0], dtype=jnp.int32)
    return jnp.argsort(jnp.where(flattened, places, places + flattened.shape[0])).astype(jnp.int32)

def block_mask(bucket, slot_lengths):
    width_slot = slot_sizes(bucket)
    places = jnp.arange(BLK, dtype=jnp.int32)
    segment = (places // width_slot).astype(jnp.int32)
    within = places - segment * width_slot
    slot_index = jnp.arange(SLOTS_BLK, dtype=jnp.int32)
    limits = lax.optimization_barrier(jnp.sum(jnp.where(segment[:, None] == slot_index[None, :], slot_lengths[None, :], 0), axis=1)).astype(jnp.int32)
    return (segment[:, None] == segment[None, :]) & (within < limits)[None, :]

def layer_norm(hidden, scale_vec, shift_vec):
    center = hidden - lax.optimization_barrier(jnp.mean(hidden, axis=-1, keepdims=True))
    spread = lax.optimization_barrier(jnp.mean(center * center, axis=-1, keepdims=True))
    return center * lax.rsqrt(spread + norm_epsilon) * scale_vec + shift_vec

def attend(packed):
    query_blk, key_blk, value_blk, bucket, slot_lengths = packed
    scores = jnp.einsum('qhd,khd->hqk', query_blk, key_blk, precision=lax.Precision.HIGHEST) * HD ** (-0.5)
    scores = jnp.where(block_mask(bucket, slot_lengths)[None], low_back(scores), -1e+30)
    weights = low(jax.nn.softmax(scores, axis=-1))
    return jnp.einsum('hqk,khd->qhd', weights, value_blk, precision=lax.Precision.HIGHEST)

def layer(inputs, buckets, lengths, w_query, b_query, w_key, w_value, b_value, w_out, b_out, gain_attn, shift_attn, w_in, b_in, w_back, b_back, gain_ffn, shift_ffn):
    block_shape = (BLK_DEV, BLK, H, HD)
    queries = low_back(low(matmul(inputs, w_query) + b_query)).reshape(block_shape)
    key_rows = low_back(low(matmul(inputs, w_key))).reshape(block_shape)
    value_rows = low_back(low(matmul(inputs, w_value) + b_value)).reshape(block_shape)
    mixed_heads = lax.map(jax.checkpoint(attend), (queries, key_rows, value_rows, buckets, lengths))
    mixed_heads = low_back(low(mixed_heads.reshape(TOK_DEV, D)))
    normed = layer_norm(inputs + low_back(matmul(mixed_heads, w_out) + b_out), gain_attn, shift_attn)
    hidden_pre = low_back(matmul(low(normed), w_in) + b_in)
    active = low(jax.nn.gelu(hidden_pre, approximate=False))
    return layer_norm(normed + low_back(matmul(active, w_back) + b_back), gain_ffn, shift_ffn)

def cls_positions(buckets):
    starts, inside = candidates(buckets)
    offsets = BLK * jnp.arange(BLK_DEV, dtype=jnp.int32)[:, None]
    return (starts + offsets).reshape(-1)[compact_order(inside)]

def ranking_loss(cls_all, positives):
    cls_low = low(cls_all)
    queries = cls_low[:N_BATCH].reshape(QUERIES, D)
    passages = cls_low[N_BATCH:, :PAS_DEV].reshape(PASSAGES, D)
    scores = low_back(matmul(queries, passages.T) * D ** (-0.5))
    picked = jnp.take_along_axis(scores, positives[:, None], axis=1)[:, 0]
    return jnp.sum(jax.nn.logsumexp(scores, axis=1) - picked)

def reference(tokens, buckets, lengths, positives, w_query, b_query, w_key, w_value, b_value, w_out, b_out, gain_attn, shift_attn, w_in, b_in, w_back, b_back, gain_ffn, shift_ffn):
    params = tuple((weight.astype(jnp.float32) for weight in (w_query, b_query, w_key, w_value, b_value, w_out, b_out, gain_attn, shift_attn, w_in, b_in, w_back, b_back, gain_ffn, shift_ffn)))
    token_dev = tokens.reshape(DEVICES, TOK_DEV, D)
    bucket_dev = buckets.reshape(DEVICES, BLK_DEV)
    length_dev = lengths.reshape(DEVICES, BLK_DEV, SLOTS_BLK)

    def forward(unused_carry, packed):
        inputs, bucket_here, length_here = packed
        output = layer(inputs.astype(jnp.float32), bucket_here, length_here, *params)
        return (unused_carry, (output.astype(jnp.bfloat16), output[cls_positions(bucket_here)]))
    kept_carry, outputs = lax.scan(forward, jnp.zeros((), jnp.float32), (token_dev, bucket_dev, length_dev))
    encoded, cls_all = outputs

    def loss_of(cls_values):
        return ranking_loss(cls_values, positives)
    kept_loss, pull_loss = jax.vjp(loss_of, cls_all)
    cls_grads = pull_loss(jnp.ones((), jnp.float32))[0]

    def backward(running, packed):
        inputs, bucket_here, length_here, grad_here = packed

        def local_layer(inputs_f, *weights):
            return layer(inputs_f, bucket_here, length_here, *weights)
        output, pull_layer = jax.vjp(local_layer, inputs.astype(jnp.float32), *params)
        output_grad = jnp.zeros_like(output).at[cls_positions(bucket_here)].add(grad_here)
        gradients = pull_layer(output_grad)
        return (tuple((summed + gradient for summed, gradient in zip(running, gradients[1:]))), gradients[0])
    totals, tokens_grad = lax.scan(backward, tuple((jnp.zeros_like(weight) for weight in params)), (token_dev, bucket_dev, length_dev, cls_grads))
    return (encoded.reshape(TOKENS, D), tokens_grad.reshape(TOKENS, D), totals[0], totals[1], totals[2], totals[3], totals[4], totals[5], totals[6], totals[7], totals[8], totals[9], totals[10], totals[11], totals[12], totals[13], totals[14])
```

```python
import functools
import typing

import jax
import jax.numpy as jnp
from jax import lax
from jax.experimental import pallas as pl
from jax.experimental.pallas import tpu as pltpu
from jax.sharding import PartitionSpec as P

H = 12
HD = 64
QLEN = 32
SHORT = 128
LONG = 256
BLK = 512
SLOTS_BLK = 16
PAS_DEV = 6


norm_epsilon = 1e-06


def matmul(left, right):
    return jnp.dot(left, right, preferred_element_type=jnp.float32)


def matmul_tn(left, right):
    return lax.dot_general(
        left, right, (((0,), (0,)), ((), ())), preferred_element_type=jnp.float32
    )


def matmul_nt(left, right):
    return lax.dot_general(
        left, right, (((1,), (1,)), ((), ())), preferred_element_type=jnp.float32
    )


def gelu_exact(values):
    return jax.nn.gelu(values, approximate=False)


def slot_sizes(buckets):
    return jnp.where(buckets == 0, QLEN, jnp.where(buckets == 1, SHORT, LONG)).astype(jnp.int32)


def candidates(buckets):
    sizes_here = slot_sizes(buckets)
    slot_index = jnp.arange(SLOTS_BLK, dtype=jnp.int32)
    starts = slot_index[None, :] * sizes_here[:, None]
    inside = starts < BLK
    return (jnp.where(inside, starts, 0), inside)


def compact_order(inside):
    flattened = inside.reshape(-1)
    places = jnp.arange(flattened.shape[0], dtype=jnp.int32)
    return jnp.argsort(jnp.where(flattened, places, places + flattened.shape[0]))


def block_mask(bucket, slot_lengths):
    width_slot = slot_sizes(bucket)
    places = jnp.arange(BLK, dtype=jnp.int32)
    segment = places // width_slot
    within = places - segment * width_slot
    slot_index = jnp.arange(SLOTS_BLK, dtype=jnp.int32)
    limits = jnp.sum(
        jnp.where(segment[:, None] == slot_index[None, :], slot_lengths[None, :], 0), axis=1
    )
    return (segment[:, None] == segment[None, :]) & (within < limits)[None, :]


def layer_norm(hidden, scale_vec, shift_vec):
    center = hidden - jnp.mean(hidden, axis=-1, keepdims=True)
    spread = jnp.mean(center * center, axis=-1, keepdims=True)
    return center * lax.rsqrt(spread + norm_epsilon) * scale_vec + shift_vec


def rank_gradient(query_block, passages, picked, score_scale):
    scores = matmul_nt(query_block, passages) * score_scale
    targets = (jnp.arange(passages.shape[0], dtype=jnp.int32)[None, :] == picked[:, None]).astype(
        jnp.float32
    )
    return (jax.nn.softmax(scores, axis=1) - targets).astype(jnp.bfloat16)


def plain_shards(
    tokens,
    buckets,
    lengths,
    positives,
    w_query,
    b_query,
    w_key,
    w_value,
    b_value,
    w_out,
    b_out,
    gain_attn,
    shift_attn,
    w_in,
    b_in,
    w_back,
    b_back,
    gain_ffn,
    shift_ffn,
):
    tok_rows = tokens.shape[0]
    width = tokens.shape[1]
    blocks = tok_rows // BLK
    block_shape = (blocks, BLK, H, HD)
    head_scale = HD ** (-0.5)
    inputs = tokens.astype(jnp.float32)
    query_rows = (matmul(tokens, w_query) + b_query).astype(jnp.bfloat16)
    key_rows = matmul(tokens, w_key).astype(jnp.bfloat16)
    value_rows = (matmul(tokens, w_value) + b_value).astype(jnp.bfloat16)

    def attend(packed):
        query_blk, key_blk, value_blk, bucket, slot_lengths = packed
        scores = (
            jnp.einsum("qhd,khd->hqk", query_blk, key_blk, preferred_element_type=jnp.float32)
            * head_scale
        )
        scores = jnp.where(block_mask(bucket, slot_lengths)[None], scores, -1e30)
        highest = jnp.max(scores, axis=-1, keepdims=True)
        raised = jnp.exp(scores - highest)
        row_totals = jnp.sum(raised, axis=-1, keepdims=True)
        weights = (raised / row_totals).astype(jnp.bfloat16)
        mixed_blk = jnp.einsum(
            "hqk,khd->qhd", weights, value_blk, preferred_element_type=jnp.float32
        )
        return (mixed_blk.astype(jnp.bfloat16), (highest + jnp.log(row_totals))[..., 0])

    mixed_heads, log_totals = lax.map(
        attend,
        (
            query_rows.reshape(block_shape),
            key_rows.reshape(block_shape),
            value_rows.reshape(block_shape),
            buckets,
            lengths,
        ),
    )
    mixed_heads = mixed_heads.reshape(tok_rows, width)
    hidden_one = inputs + matmul(mixed_heads, w_out) + b_out
    normed = layer_norm(hidden_one, gain_attn, shift_attn)
    normed_low = normed.astype(jnp.bfloat16)
    hidden_pre = matmul(normed_low, w_in) + b_in
    active = gelu_exact(hidden_pre).astype(jnp.bfloat16)
    hidden_two = normed + matmul(active, w_back) + b_back
    output = layer_norm(hidden_two, gain_ffn, shift_ffn)
    encoded = output.astype(jnp.bfloat16)
    slot_starts, inside = candidates(buckets)
    cand_rows = (slot_starts + BLK * jnp.arange(blocks, dtype=jnp.int32)[:, None]).reshape(-1)
    order_index = compact_order(inside)
    inverse_index = jnp.argsort(order_index)
    cls_count = cand_rows.shape[0]
    cls_mine = output[cand_rows[order_index]].astype(jnp.bfloat16)
    groups = lax.axis_size("grp")
    members = lax.axis_size("batch")
    group_here = lax.axis_index("grp")
    member_here = lax.axis_index("batch")
    gathered = lax.all_gather(cls_mine, ("grp", "batch"), axis=0, tiled=True).reshape(
        groups, members, cls_count, width
    )
    queries = gathered[0].reshape(members * cls_count, width)
    passages = gathered[1:, :, :PAS_DEV].reshape((groups - 1) * members * PAS_DEV, width)
    score_scale = width ** (-0.5)
    query_share = cls_count // groups
    first_query = member_here * cls_count + group_here * query_share
    own_queries = lax.dynamic_slice_in_dim(queries, first_query, query_share, 0)
    own_picked = lax.dynamic_slice_in_dim(positives, first_query, query_share, 0)
    rank_grad = rank_gradient(own_queries, passages, own_picked, score_scale)
    query_part = matmul(rank_grad, passages) * score_scale
    query_rows_grad = lax.all_gather(query_part, "grp", axis=0, tiled=True)
    passage_terms = jnp.concatenate(
        [
            jnp.zeros((members * PAS_DEV, width), jnp.float32),
            matmul_tn(rank_grad, own_queries) * score_scale,
        ],
        axis=0,
    )
    passage_rows_grad = lax.psum_scatter(
        passage_terms, ("grp", "batch"), scatter_dimension=0, tiled=True
    )
    padded_passage = jnp.pad(passage_rows_grad, ((0, cls_count - PAS_DEV), (0, 0)))
    cls_grad = jnp.where(group_here == 0, query_rows_grad, padded_passage)
    output_grad = cls_grad[inverse_index]
    kept_two, pull_two = jax.vjp(layer_norm, hidden_two[cand_rows], gain_ffn, shift_ffn)
    two_grad, gain_ffn_grad, shift_ffn_grad = pull_two(output_grad)
    branch_grad = two_grad.astype(jnp.bfloat16)
    b_back_grad = jnp.sum(branch_grad.astype(jnp.float32), axis=0)
    w_back_grad = matmul_tn(active[cand_rows], branch_grad)
    kept_gelu, pull_gelu = jax.vjp(gelu_exact, hidden_pre[cand_rows])
    pre_grad = pull_gelu(matmul_nt(branch_grad, w_back))[0].astype(jnp.bfloat16)
    b_in_grad = jnp.sum(pre_grad.astype(jnp.float32), axis=0)
    w_in_grad = matmul_tn(normed_low[cand_rows], pre_grad)
    normed_grad = two_grad + matmul_nt(pre_grad, w_in)
    kept_one, pull_one = jax.vjp(layer_norm, hidden_one[cand_rows], gain_attn, shift_attn)
    one_grad, gain_attn_grad, shift_attn_grad = pull_one(normed_grad)
    attn_grad = one_grad.astype(jnp.bfloat16)
    b_out_grad = jnp.sum(attn_grad.astype(jnp.float32), axis=0)
    w_out_grad = matmul_tn(mixed_heads[cand_rows], attn_grad)
    mixed_grad = matmul_nt(attn_grad, w_out).astype(jnp.bfloat16)
    slots_block = slot_starts.shape[1]
    row_shape = (blocks, slots_block, H, HD)
    query_cls = query_rows[cand_rows].reshape(row_shape)
    mixed_cls = mixed_grad.reshape(row_shape)
    log_cls = jnp.take_along_axis(
        log_totals, jnp.broadcast_to(slot_starts[:, None, :], (blocks, H, slots_block)), axis=2
    )

    def attend_back(packed):
        query_blk, key_blk, value_blk, grad_blk, log_blk, bucket, slot_lengths, start_blk = packed
        visible = block_mask(bucket, slot_lengths)[start_blk]
        scores_blk = (
            jnp.einsum("shd,khd->hsk", query_blk, key_blk, preferred_element_type=jnp.float32)
            * head_scale
        )
        scores_blk = jnp.where(visible[None], scores_blk, -1e30)
        weights = jnp.exp(scores_blk - log_blk[..., None])
        value_back = jnp.einsum(
            "hsk,shd->khd",
            weights.astype(jnp.bfloat16),
            grad_blk,
            preferred_element_type=jnp.float32,
        )
        weight_grad = jnp.einsum(
            "shd,khd->hsk", grad_blk, value_blk, preferred_element_type=jnp.float32
        )
        score_back = (
            weights * (weight_grad - jnp.sum(weights * weight_grad, axis=-1, keepdims=True))
        ).astype(jnp.bfloat16)
        query_back = (
            jnp.einsum("hsk,khd->shd", score_back, key_blk, preferred_element_type=jnp.float32)
            * head_scale
        )
        key_back = (
            jnp.einsum("hsk,shd->khd", score_back, query_blk, preferred_element_type=jnp.float32)
            * head_scale
        )
        return (query_back, key_back, value_back)

    query_back, key_back, value_back = lax.map(
        attend_back,
        (
            query_cls,
            key_rows.reshape(block_shape),
            value_rows.reshape(block_shape),
            mixed_cls,
            log_cls,
            buckets,
            lengths,
            slot_starts,
        ),
    )
    query_back = query_back.reshape(cls_count, width).astype(jnp.bfloat16)
    key_back = key_back.reshape(tok_rows, width).astype(jnp.bfloat16)
    value_back = value_back.reshape(tok_rows, width).astype(jnp.bfloat16)
    b_query_grad = jnp.sum(query_back.astype(jnp.float32), axis=0)
    w_query_grad = matmul_tn(tokens[cand_rows], query_back)
    w_key_grad = matmul_tn(tokens, key_back)
    w_value_grad = matmul_tn(tokens, value_back)
    b_value_grad = jnp.sum(value_back.astype(jnp.float32), axis=0)
    row_grad = one_grad + matmul_nt(query_back, w_query)
    tokens_grad = (
        (matmul_nt(key_back, w_key) + matmul_nt(value_back, w_value)).at[cand_rows].add(row_grad)
    )
    all_shares = (
        lax.psum_scatter(w_query_grad, "batch", scatter_dimension=0, tiled=True),
        lax.psum_scatter(b_query_grad, "batch", scatter_dimension=0, tiled=True),
        lax.psum_scatter(w_key_grad, "batch", scatter_dimension=0, tiled=True),
        lax.psum_scatter(w_value_grad, "batch", scatter_dimension=0, tiled=True),
        lax.psum_scatter(b_value_grad, "batch", scatter_dimension=0, tiled=True),
        lax.psum_scatter(w_out_grad, "batch", scatter_dimension=0, tiled=True),
        lax.psum_scatter(b_out_grad, "batch", scatter_dimension=0, tiled=True),
        lax.psum_scatter(gain_attn_grad, "batch", scatter_dimension=0, tiled=True),
        lax.psum_scatter(shift_attn_grad, "batch", scatter_dimension=0, tiled=True),
        lax.psum_scatter(w_in_grad, "batch", scatter_dimension=0, tiled=True),
        lax.psum_scatter(b_in_grad, "batch", scatter_dimension=0, tiled=True),
        lax.psum_scatter(w_back_grad, "batch", scatter_dimension=0, tiled=True),
        lax.psum_scatter(b_back_grad, "batch", scatter_dimension=0, tiled=True),
        lax.psum_scatter(gain_ffn_grad, "batch", scatter_dimension=0, tiled=True),
        lax.psum_scatter(shift_ffn_grad, "batch", scatter_dimension=0, tiled=True),
    )
    summed = tuple(
        lax.psum(
            (
                all_shares[0],
                all_shares[1],
                all_shares[2],
                all_shares[3],
                all_shares[4],
                all_shares[5],
                all_shares[6],
                all_shares[7],
                all_shares[8],
                all_shares[9],
                all_shares[10],
                all_shares[11],
                all_shares[12],
                all_shares[13],
                all_shares[14],
            ),
            "grp",
        )
    )
    return (
        encoded,
        tokens_grad,
        summed[0],
        summed[1],
        summed[2],
        summed[3],
        summed[4],
        summed[5],
        summed[6],
        summed[7],
        summed[8],
        summed[9],
        summed[10],
        summed[11],
        summed[12],
        summed[13],
        summed[14],
    )


MESH = pl.DeviceIdType.MESH
HEADS_VREG = 4
PART = 16


def nn(left, right):
    return lax.dot_general(
        left, right, (((1,), (0,)), ((), ())), preferred_element_type=jnp.float32
    )


def nt(left, right):
    return lax.dot_general(
        left, right, (((1,), (1,)), ((), ())), preferred_element_type=jnp.float32
    )


def tn(left, right):
    return lax.dot_general(
        left, right, (((0,), (0,)), ((), ())), preferred_element_type=jnp.float32
    )


def low(values):
    return values.astype(jnp.bfloat16)


def wide(values):
    return values.astype(jnp.float32)


def iota(shape, axis):
    return lax.broadcasted_iota(jnp.int32, shape, axis)


def gelu(values):
    middle = 0.5 * values
    return middle + middle * lax.erf(values * 0.7071067811865476)


def gelu_slope(values):
    below = 0.5 + 0.5 * lax.erf(values * 0.7071067811865476)
    return below + values * (0.3989422804014327 * jnp.exp(-0.5 * (values * values)))


def gelu_both(values):
    below = 0.5 + 0.5 * lax.erf(values * 0.7071067811865476)
    bell = 0.3989422804014327 * jnp.exp(-0.5 * (values * values))
    return values * below, below + values * bell


def unit_rows(hidden):
    center = hidden - jnp.mean(hidden, axis=-1, keepdims=True)
    rate = lax.rsqrt(jnp.mean(center * center, axis=-1, keepdims=True) + norm_epsilon)
    return center * rate, rate


def norm_back(grad, unit, rate, gain):
    scaled = grad * gain
    return rate * (
        scaled
        - jnp.mean(scaled, axis=-1, keepdims=True)
        - unit * jnp.mean(scaled * unit, axis=-1, keepdims=True)
    )


def hold(sem, ref):
    pltpu.make_async_copy(ref, ref, sem).wait()


def pack_eight(values):
    middle = values.shape[1] // 2
    values = wide(values)
    return low(jnp.concatenate([values[:, :middle], values[:, middle:]], axis=0))


def unpack_eight(values):
    count, _, middle = values.shape
    values = wide(values)
    return jnp.concatenate(
        [values[:, 0:8].reshape(8 * count, middle), values[:, 8:16].reshape(8 * count, middle)], axis=1
    )


class Ins(typing.NamedTuple):
    tokens: typing.Any
    buckets: typing.Any
    lengths: typing.Any
    positives: typing.Any
    w_query: typing.Any
    b_query: typing.Any
    w_key: typing.Any
    w_value: typing.Any
    b_value: typing.Any
    w_out: typing.Any
    b_out: typing.Any
    gain_attn: typing.Any
    shift_attn: typing.Any
    w_in: typing.Any
    b_in: typing.Any
    w_back: typing.Any
    b_back: typing.Any
    gain_ffn: typing.Any
    shift_ffn: typing.Any


class Outs(typing.NamedTuple):
    encoded: typing.Any
    left_out: typing.Any
    right_out: typing.Any
    g_query: typing.Any
    gb_query: typing.Any
    g_key: typing.Any
    g_value: typing.Any
    gb_value: typing.Any
    g_out: typing.Any
    gb_out: typing.Any
    g_gain_attn: typing.Any
    g_shift_attn: typing.Any
    g_in: typing.Any
    gb_in: typing.Any
    g_back: typing.Any
    gb_back: typing.Any
    g_gain_ffn: typing.Any
    g_shift_ffn: typing.Any


class Scratch(typing.NamedTuple):
    tokens_v: typing.Any
    w_query_v: typing.Any
    w_key_v: typing.Any
    w_value_v: typing.Any
    w_out_v: typing.Any
    w_in_v: typing.Any
    w_back_v: typing.Any
    vectors_v: typing.Any
    b_in_1d: typing.Any
    vector_sem: typing.Any
    rows_v: typing.Any
    t_sum: typing.Any
    b_in_v: typing.Any
    key_seg: typing.Any
    left: typing.Any
    right: typing.Any
    prob: typing.Any
    slope: typing.Any
    unit_one: typing.Any
    rate_one: typing.Any
    unit_two: typing.Any
    rate_two: typing.Any
    cls: typing.Any
    y_grad: typing.Any
    x_all: typing.Any
    mixed_all: typing.Any
    normed_all: typing.Any
    branch_all: typing.Any
    attn_all: typing.Any
    query_all: typing.Any
    few_all: typing.Any
    few_out: typing.Any
    t_side: typing.Any
    u_side: typing.Any
    u_twin: typing.Any
    t_few: typing.Any
    u_few: typing.Any
    side_got: typing.Any
    few_got: typing.Any
    sum_out: typing.Any
    sum_in: typing.Any
    pas_out: typing.Any
    pas_in: typing.Any
    pas_part: typing.Any
    pas_twin: typing.Any
    pas_sum: typing.Any
    pas_got: typing.Any
    normed_v: typing.Any
    enc_v: typing.Any
    flat_a: typing.Any
    flat_b: typing.Any
    flat_c: typing.Any
    flat_d: typing.Any
    factor: typing.Any
    stage: typing.Any
    swap_out0: typing.Any
    swap_in0: typing.Any
    swap_out1: typing.Any
    swap_in1: typing.Any
    load_sem: typing.Any
    store_sem: typing.Any
    g_send: typing.Any
    g_recv: typing.Any
    f_send: typing.Any
    f_recv: typing.Any
    v_send: typing.Any
    v_recv: typing.Any
    a_send: typing.Any
    a_recv: typing.Any
    b_send: typing.Any
    b_recv: typing.Any
    s_send: typing.Any
    s_recv: typing.Any


class Refs:
    pass


X_ALL, MIXED_ALL, NORMED_ALL, BRANCH_ALL, ATTN_ALL, QUERY_ALL, FEW_ALL, LAST_ALL = range(8)
TO_QUERY = (X_ALL, NORMED_ALL, BRANCH_ALL, QUERY_ALL)
TO_PASSAGE = (MIXED_ALL, NORMED_ALL, BRANCH_ALL, ATTN_ALL)
EARLY, LATE = range(2)
B_QUERY, B_VALUE, B_OUT, GAIN_ATTN, SHIFT_ATTN, B_BACK, GAIN_FFN, SHIFT_FFN = range(8)
W_QUERY, W_KEY, W_VALUE, W_OUT, W_IN, W_BACK, TOKENS = range(7)


def main_kernel(sizes, *refs):
    groups, members, rows, width, hidden = sizes
    r = Refs()
    ends = (len(Ins._fields), len(Ins._fields) + len(Outs._fields))
    for group in (Ins(*refs[: ends[0]]), Outs(*refs[ends[0] : ends[1]]), Scratch(*refs[ends[1] :])):
        r.__dict__.update(group._asdict())
    across = members // 8
    depth = 4
    share = width // members
    cand = rows // QLEN
    lanes = H * cand
    slots = members
    query_rows = slots * cand
    all_rows = query_rows + slots * 8
    half = width // 2
    score_scale = width ** (-0.5)

    grp = lax.axis_index("grp")
    bat = lax.axis_index("batch")
    core = lax.rem(bat, 2)
    col = lax.rem(lax.div(bat, 2), across)
    lay = lax.div(bat, 2 * across)
    sibling = bat + 1 - 2 * core
    is_query = grp == 0
    is_passage = grp > 0

    def slot_of(member):
        return (
            lax.rem(member, 2) * across + lax.rem(lax.div(member, 2), across)
        ) * depth + lax.div(member, 2 * across)

    my_slot = slot_of(bat)

    weights = (r.w_query, r.w_key, r.w_value, r.w_out, r.w_in, r.w_back, r.tokens)
    held = (r.w_query_v, r.w_key_v, r.w_value_v, r.w_out_v, r.w_in_v, r.w_back_v, r.tokens_v)

    def load(at):
        return pltpu.make_async_copy(weights[at], held[at], r.load_sem.at[at])

    load(TOKENS).start()

    vectors = (
        r.b_query,
        r.b_value,
        r.b_out,
        r.gain_attn,
        r.shift_attn,
        r.b_back,
        r.gain_ffn,
        r.shift_ffn,
    )
    vector_loads = [
        pltpu.make_async_copy(vector, r.vectors_v.at[at], r.vector_sem.at[at]) for at, vector in enumerate(vectors)
    ]
    vector_loads.append(pltpu.make_async_copy(r.b_in, r.b_in_1d, r.vector_sem.at[len(vectors)]))
    for copy in vector_loads:
        copy.start()
    for at in (W_QUERY, W_KEY):
        load(at).start()

    barrier = pltpu.get_barrier_semaphore()

    def greet(step, carry):
        other = lax.rem(bat + step, members)

        @pl.when(step > 0)
        def _():
            pl.semaphore_signal(barrier, inc=1, device_id=(grp, other), device_id_type=MESH)

        pl.semaphore_signal(barrier, inc=1, device_id=(1 - grp, other), device_id_type=MESH)
        return carry

    lax.fori_loop(0, members, greet, 0)

    def remote(src, dst, send, recv, to):
        return pltpu.make_async_remote_copy(
            src_ref=src, dst_ref=dst, send_sem=send, recv_sem=recv, device_id=to, device_id_type=MESH
        )

    def vec(at):
        return r.rows_v[at : at + 1, :]

    def bucket_of(block):
        return r.buckets[block]

    def size_of(bucket):
        return jnp.where(bucket == 0, QLEN, jnp.where(bucket == 1, SHORT, LONG))

    def count_of(bucket):
        return jnp.where(bucket == 0, BLK // QLEN, jnp.where(bucket == 1, BLK // SHORT, BLK // LONG))

    first, second = bucket_of(0), bucket_of(1)
    first_count, second_count = count_of(first), count_of(second)

    def listed(index):
        later = index - first_count
        inside = index < first_count + second_count
        place = jnp.where(index < first_count, index * size_of(first), BLK + later * size_of(second))
        segment = jnp.where(index < first_count, index, SLOTS_BLK + later)
        return jnp.where(inside, place, -1), jnp.where(inside, segment, -2)

    def segment_of(token, bucket):
        within = token & (BLK - 1)
        slot = jnp.where(
            bucket == 0, within >> 5, jnp.where(bucket == 1, within >> 7, within >> 8)
        )
        place = jnp.where(
            bucket == 0, within & (QLEN - 1), jnp.where(bucket == 1, within & (SHORT - 1), within & (LONG - 1))
        )
        return slot + SLOTS_BLK * (token >> 9), place

    token = iota((1, rows), 1)
    bucket_row = jnp.where(token < BLK, first, second)
    segment_row, place_row = segment_of(token, bucket_row)
    limit_row = jnp.zeros((1, rows), jnp.int32)
    for at in range(rows // BLK * SLOTS_BLK):
        used = r.lengths[at // SLOTS_BLK, at % SLOTS_BLK]
        limit_row = jnp.where(segment_row == at, used, limit_row)
    key_segment = jnp.where(place_row < limit_row, segment_row, -1)
    for at in range(rows // 256):
        r.key_seg[at] = key_segment[:, 256 * at : 256 * at + 256]

    lane_head = iota((cand, width), 1) >> 6

    def by_head(values):
        values = wide(values)
        return low(
            jnp.concatenate([jnp.where(lane_head == h, values, 0.0) for h in range(H)], axis=0)
        )

    def pick_heads(values):
        total = jnp.zeros((cand, width), jnp.float32)
        for h in range(H):
            total = total + jnp.where(lane_head == h, values[h * cand : (h + 1) * cand], 0.0)
        return total

    gathered = (r.x_all, r.mixed_all, r.normed_all, r.branch_all, r.attn_all, r.query_all, r.few_all.at[EARLY], r.few_all.at[LATE])

    def keep(name, values):
        @pl.when(is_query)
        def _():
            gathered[name][core, col, lay, 0:cand] = values[:, :half]
            gathered[name][core, col, lay, cand : 2 * cand] = values[:, half:]

        @pl.when(is_passage)
        def _():
            packed = pack_eight(values[0:8])
            if name in TO_QUERY:
                when, at = divmod(TO_QUERY.index(name), 2)
                r.few_out[when, PART * at : PART * at + PART] = packed
            if name in TO_PASSAGE:
                when, at = divmod(TO_PASSAGE.index(name), 2)
                r.few_all[when, core, col, lay, PART * at : PART * at + PART] = packed

    def few_rows(values):
        eight = values.reshape(H, cand, width)[:, 0:8].reshape(8 * H, width)
        return low(jnp.concatenate([eight, jnp.zeros((128 - 8 * H, width), jnp.float32)], axis=0).T)

    def goes_to(name):
        if name == FEW_ALL or name in TO_QUERY and name in TO_PASSAGE:
            return grp >= 0
        return is_query if name in TO_QUERY else is_passage

    def sems(name, stage):
        return r.g_send.at[name, stage], r.g_recv.at[name, stage]

    def my_piece(name):
        return gathered[name].at[core, col, lay]

    def go(name, stage):
        buf = gathered[name]
        send, recv = sems(name, stage)
        if stage == 0:

            @pl.when(is_passage if name == FEW_ALL else is_query)
            def _():
                src = r.few_out.at[EARLY] if name == FEW_ALL else my_piece(name)
                remote(src, my_piece(name), send, recv, (1 - grp, bat)).start()

            return

        @pl.when(goes_to(name))
        def _():
            if stage == 1:
                piece = my_piece(name)
                for ahead in range(1, depth):
                    to = (lax.rem(lay + ahead, depth) * across + col) * 2 + core
                    remote(piece, piece, send, recv, (grp, to)).start()
            elif stage == 2:
                piece = buf.at[core, col]
                for ahead in range(1, across):
                    to = (lay * across + lax.rem(col + ahead, across)) * 2 + core
                    remote(piece, piece, send, recv, (grp, to)).start()
            else:
                piece = buf.at[core]
                remote(piece, piece, send, recv, (grp, sibling)).start()

    def size_waits(name, stage, side):
        buf = gathered[name]
        sem = sems(name, stage)[side]
        if stage == 0:
            if name == FEW_ALL or name in TO_PASSAGE:

                @pl.when(is_passage if (name == FEW_ALL) == (side == 0) else is_query)
                def _():
                    hold(sem, my_piece(name))

            return

        @pl.when(goes_to(name))
        def _():
            if stage == 1:
                hold(sem, buf.at[core, col, pl.ds(0, depth - 1)])
            elif stage == 2:
                hold(sem, buf.at[core, pl.ds(0, across - 1)])
            else:
                hold(sem, buf.at[core])

    def come(name, stage):
        size_waits(name, stage, 1)

    def sent(name):
        for stage in range(4):
            size_waits(name, stage, 0)

    def step_on(name, stage):
        come(name, stage - 1)
        go(name, stage)

    def few_go():
        @pl.when(is_passage)
        def _():
            dst = r.few_all.at[LATE, core, col, lay]

            def push(step, carry):
                other = lax.rem(bat + 2 * step, members)
                remote(r.few_out.at[LATE], dst, r.f_send.at[0], r.f_recv.at[0], (0, other)).start()
                return carry

            lax.fori_loop(0, members // 2, push, 0)

    def few_turn():
        whole = r.few_all.at[LATE, core]
        hold(r.f_recv.at[0], whole)
        remote(whole, whole, r.f_send.at[1], r.f_recv.at[1], (grp, sibling)).start()

    def few_come():
        @pl.when(is_query)
        def _():
            hold(r.f_recv.at[1], r.few_all.at[LATE, core])

        come(LAST_ALL, 3)

    def few_sent():
        @pl.when(is_query)
        def _():
            hold(r.f_send.at[1], r.few_all.at[LATE, core])

        @pl.when(is_passage)
        def _():
            hold(r.f_send.at[0], r.few_all.at[LATE, core])

    def share_rows(member):
        return pl.ds(pl.multiple_of(member * share, share), share)

    def spread(src, dst, at, to_grp, first_step, end_step=members):
        send, recv = r.a_send.at[at], r.a_recv.at[at]

        def push(step, carry):
            other = lax.rem(bat + step, members)
            remote(src(share_rows(other)), dst(my_slot), send, recv, (to_grp, other)).start()
            return carry

        lax.fori_loop(first_step, end_step, push, 0)

    def spread_t(first_step, end_step):
        spread(lambda rows: r.t_side.at[:, rows], lambda slot: r.side_got.at[slot], 0, 0, first_step, end_step)

    def sum_peer(step):
        if step == 0:
            return (1 - grp, bat)
        if step in (1, 2):
            other = lay + 1 - 2 * lax.rem(lay, 2) if step == 1 else lax.rem(lay + 2, depth)
            return (grp, (other * across + col) * 2 + core)
        if step == 3:
            return (grp, (lay * across + 1 - col) * 2 + core)
        return (grp, sibling)

    def sum_go(step):
        remote(
            r.sum_out.at[step], r.sum_in.at[step], r.v_send.at[step], r.v_recv.at[step], sum_peer(step)
        ).start()

    def sum_come(step):
        hold(r.v_recv.at[step], r.sum_in.at[step])
        r.sum_out[step + 1] = r.sum_out[step] + r.sum_in[step]

    load(TOKENS).wait()
    for at in (W_VALUE, W_OUT, W_IN, W_BACK):
        load(at).start()
    for copy in vector_loads:
        copy.wait()
    for at in range(len(vectors)):
        r.rows_v[at : at + 1, :] = r.vectors_v[at].reshape(1, width)
    r.b_in_v[...] = r.b_in_1d[...].reshape(1, hidden)
    place_col, _ = listed(iota((cand, 1), 0))
    _, seg_col = listed(iota((lanes, 1), 0) & (cand - 1))
    tokens_v = r.tokens_v
    pick = low(jnp.where(iota((cand, rows), 1) == place_col, 1.0, 0.0))
    r.left[2 * lanes : 2 * lanes + cand, :] = pick
    r.left[2 * lanes + cand : 2 * lanes + 2 * cand, :] = pick
    x_cls = nn(pick, tokens_v[...])
    x_low = low(x_cls)
    keep(X_ALL, x_low)
    pl.semaphore_wait(barrier, 2 * members - 1)
    go(X_ALL, 1)
    load(W_QUERY).wait()
    load(W_KEY).wait()
    q_cls = by_head(low(nn(x_low, r.w_query_v[...]) + vec(B_QUERY)))
    key_query = low(nt(q_cls, r.w_key_v[...]) * HD ** (-0.5))
    r.right[lanes : 2 * lanes, :] = key_query
    scores = nt(key_query, tokens_v[...])
    scores = jnp.where(seg_col == key_segment, scores, -1e30)
    raised = jnp.exp(scores - jnp.max(scores, axis=-1, keepdims=True))
    prob = raised / jnp.sum(raised, axis=-1, keepdims=True)
    r.prob[...] = prob
    r.left[0:lanes, :] = low(prob)
    value_sum = nn(r.left[0:lanes, :], tokens_v[...])
    @pl.when(is_query)
    def _():
        for v in range(lanes // 128):
            r.u_side[v] = low(value_sum[128 * v : 128 * v + 128].T)
        spread(lambda rows: r.u_side.at[pl.ds(0, 2), rows], lambda slot: r.side_got.at[slot, pl.ds(0, 2)], 4, 1, 0)

    @pl.when(is_passage)
    def _():
        r.u_few[...] = few_rows(value_sum)
        spread(lambda rows: r.u_few.at[rows], lambda slot: r.few_got.at[slot], 3, 1, 1)

    load(W_VALUE).wait()
    load(W_OUT).wait()
    mixed = low(pick_heads(nn(low(value_sum), r.w_value_v[...])) + vec(B_VALUE))
    keep(MIXED_ALL, mixed)
    unit_one, rate_one = unit_rows(x_cls + nn(mixed, r.w_out_v[...]) + vec(B_OUT))
    normed = unit_one * vec(GAIN_ATTN) + vec(SHIFT_ATTN)
    normed_low = low(normed)
    keep(NORMED_ALL, normed_low)
    r.unit_one[...] = unit_one
    r.rate_one[...] = rate_one
    load(W_IN).wait()
    load(W_BACK).wait()
    active, slope = gelu_both(nn(normed_low, r.w_in_v[...]) + r.b_in_v[...])
    r.slope[...] = slope
    unit_two, rate_two = unit_rows(normed + nn(low(active), r.w_back_v[...]) + vec(B_BACK))
    r.unit_two[...] = unit_two
    r.rate_two[...] = rate_two
    cls = low(unit_two * vec(GAIN_FFN) + vec(SHIFT_FFN))
    r.cls[...] = cls


    per_core = (groups - 1) * members // 2
    lanes_n = 2 * per_core * 8

    @pl.when(is_passage)
    def _():
        r.pas_out[...] = pack_eight(cls[0:8])

        def push(k, carry):
            at = (grp - 1) * (members // 2) + lax.div(bat, 2)
            remote(
                r.pas_out, r.pas_in.at[core, at], r.b_send.at[0], r.b_recv.at[0], (0, 2 * k + core)
            ).start()
            return carry

        lax.fori_loop(0, members // 2, push, 0)

    for name in (NORMED_ALL, MIXED_ALL):
        go(name, 0)
    go(FEW_ALL, 0)


    def rank_rows():
        hold(r.b_recv.at[0], r.pas_in.at[core])
        mine = r.pas_in.at[core]
        remote(mine, mine, r.b_send.at[1], r.b_recv.at[1], (grp, sibling)).start()
        pos_col = jnp.zeros((cand, 1), jnp.int32)
        row = iota((cand, 1), 0)
        for s in range(cand):
            pos_col = jnp.where(row == s, r.positives[bat * cand + s], pos_col)
        spot = iota((1, lanes_n), 1)
        within = spot & 7
        owner = spot >> 3
        owner_core = lax.div(owner, per_core)
        owner = owner - owner_core * per_core
        owner_grp = lax.div(owner, members // 2)
        owner = (owner - owner_grp * (members // 2)) * 2 + owner_core + owner_grp * members
        real = within < PAS_DEV
        number = jnp.where(real, owner * PAS_DEV + within, -1)
        hold(r.b_recv.at[1], r.pas_in.at[1 - core])
        passages = low(unpack_eight(r.pas_in[...].reshape(2 * per_core, PART, half)))
        queries = r.cls[...]
        ranks = jnp.where(real, nt(queries, passages) * score_scale, -1e30)
        grown = jnp.exp(ranks - jnp.max(ranks, axis=-1, keepdims=True))
        soft = grown / jnp.sum(grown, axis=-1, keepdims=True)
        rank_grad = low(jnp.where(real, soft - jnp.where(number == pos_col, 1.0, 0.0), 0.0))
        r.y_grad[...] = nn(rank_grad, passages) * score_scale
        terms = (tn(rank_grad, queries) * score_scale).reshape(2 * per_core, 8, width)
        r.pas_part[...] = low(
            jnp.concatenate([terms[:, :, :half], terms[:, :, half:]], axis=1)
        ).reshape(2, per_core, PART, half)
        remote(
            r.pas_part.at[1 - core], r.pas_twin, r.b_send.at[2], r.b_recv.at[2], (grp, sibling)
        ).start()
        hold(r.b_recv.at[2], r.pas_twin)
        r.pas_sum[...] = low(wide(r.pas_part[core]) + wide(r.pas_twin[...]))

        def push(at, carry):
            to = (1 + lax.div(at, members // 2), 2 * lax.rem(at, members // 2) + core)
            remote(
                r.pas_sum.at[at], r.pas_got.at[lax.div(bat, 2)], r.b_send.at[3], r.b_recv.at[3], to
            ).start()
            return carry

        lax.fori_loop(0, per_core, push, 0)

    def passage_rows():
        hold(r.b_recv.at[3], r.pas_got)
        total = jnp.sum(wide(r.pas_got[...]), axis=0)
        r.y_grad[0:8, :] = jnp.concatenate([total[0:8], total[8:16]], axis=1)
        r.y_grad[8:cand, :] = jnp.zeros((cand - 8, width), jnp.float32)

    def backward_rows():
        y_grad = r.y_grad[...]
        unit = r.unit_two[...]
        gain_sum = jnp.sum(y_grad * unit, axis=0, keepdims=True)
        shift_sum = jnp.sum(y_grad, axis=0, keepdims=True)
        two_grad = norm_back(y_grad, unit, r.rate_two[...], vec(GAIN_FFN))
        branch = low(two_grad)
        keep(BRANCH_ALL, branch)
        go(BRANCH_ALL, 0)

        @pl.when(is_query)
        def _():
            go(BRANCH_ALL, 1)

        pre_grad = low(nt(branch, r.w_back_v[...]) * r.slope[...])
        pre_sum = jnp.sum(wide(pre_grad), axis=0, keepdims=True)
        normed_grad = two_grad + nt(pre_grad, r.w_in_v[...])
        unit = r.unit_one[...]
        gain_one = jnp.sum(normed_grad * unit, axis=0, keepdims=True)
        shift_one = jnp.sum(normed_grad, axis=0, keepdims=True)
        one_grad = norm_back(normed_grad, unit, r.rate_one[...], vec(GAIN_ATTN))
        attn = low(one_grad)
        keep(ATTN_ALL, attn)
        go(ATTN_ALL, 0)
        mixed_low = low(nt(attn, r.w_out_v[...]))
        mixed_grad = by_head(mixed_low)
        value_mix = low(nt(mixed_grad, r.w_value_v[...]))
        r.right[0:lanes, :] = value_mix
        prob_grad = nt(value_mix, tokens_v[...])
        prob = r.prob[...]
        score_grad = low(prob * (prob_grad - jnp.sum(prob * prob_grad, axis=-1, keepdims=True)))
        r.left[lanes : 2 * lanes, :] = score_grad
        token_sum = nn(score_grad, tokens_v[...])
        query_grad = low(pick_heads(nn(low(token_sum), r.w_key_v[...])) * HD ** (-0.5))
        keep(QUERY_ALL, query_grad)
        go(QUERY_ALL, 1)
        few_go()
        r.t_sum[...] = token_sum
        col_sums = [jnp.sum(wide(v), axis=0, keepdims=True) for v in (query_grad, mixed_low, attn, branch)]
        r.sum_out[0] = jnp.concatenate(
            [gain_sum, shift_sum, gain_one, shift_one]
            + col_sums
            + [pre_sum[:, width * j : width * (j + 1)] for j in range(hidden // width)]
            + [jnp.zeros((8 - hidden // width, width), jnp.float32)],
            axis=0,
        )
        sum_go(0)

        @pl.when(is_query)
        def _():
            remote(r.u_side.at[2], r.u_twin, r.a_send.at[2], r.a_recv.at[2], (1, bat)).start()

        row_grad = one_grad + nt(query_grad, r.w_query_v[...])
        row_high = low(row_grad)
        r.right[2 * lanes : 2 * lanes + cand, :] = row_high
        r.right[2 * lanes + cand : 2 * lanes + 2 * cand, :] = low(row_grad - wide(row_high))
        pltpu.make_async_copy(r.left, r.left_out, r.store_sem.at[1]).start()
        pltpu.make_async_copy(r.right, r.right_out, r.store_sem.at[2]).start()

    tile = 256
    tiles = rows // tile
    first_half = iota((1, 128), 1) < HD
    half_on = low(jnp.where(first_half, 1.0, 0.0))
    half_off = low(jnp.where(first_half, 0.0, 1.0))
    one_lanes = jnp.full((tile, 128), 1.0, jnp.bfloat16)

    def attend_tile(i):
        at = pl.multiple_of(i * tile, tile)
        tok = tokens_v[pl.ds(at, tile), :]
        query = low(nn(tok, r.w_query_v[...]) + vec(B_QUERY)) * jnp.bfloat16(HD ** (-0.5))
        key = low(nn(tok, r.w_key_v[...]))
        value = low(nn(tok, r.w_value_v[...]) + vec(B_VALUE))
        token_col = iota((tile, 1), 0) + at
        bucket = jnp.where(i < BLK // tile, first, second)
        segment, _ = segment_of(token_col, bucket)
        unseen = jnp.where(segment == r.key_seg[i], 0.0, -1e30)
        outs = []
        for pair in range(H // 2):
            span = slice(128 * pair, 128 * pair + 128)
            q_pair, k_pair, v_pair = query[:, span], key[:, span], value[:, span]
            value_one = jnp.concatenate([v_pair, one_lanes], axis=1)
            parts = []
            for side in (half_on, half_off):
                s = nt(q_pair * side, k_pair) + unseen
                e = jnp.exp(s - jnp.max(s, axis=-1, keepdims=True))
                both = nn(low(e), value_one)
                parts.append(both[:, :128] / both[:, 128:])
            outs.append(low(jnp.where(first_half, parts[0], parts[1])))
        mixed_tile = jnp.concatenate(outs, axis=1)
        unit_tile, _ = unit_rows(wide(tok) + nn(mixed_tile, r.w_out_v[...]) + vec(B_OUT))
        r.normed_v[...] = unit_tile * vec(GAIN_ATTN) + vec(SHIFT_ATTN)

    def feed_tile(i):
        at = pl.multiple_of(i * tile, tile)
        normed_tile = r.normed_v[...]
        low_tile = low(normed_tile)
        total = normed_tile + vec(B_BACK)
        span = hidden // 4
        pre = nn(low_tile, r.w_in_v[:, 0:span]) + r.b_in_v[:, 0:span]
        for j in range(4):
            ahead = slice((j + 1) * span, (j + 2) * span)
            if j < 3:
                later = nn(low_tile, r.w_in_v[:, ahead]) + r.b_in_v[:, ahead]
            total = total + nn(low(gelu(pre)), r.w_back_v[j * span : (j + 1) * span, :])
            pre = later
        unit_tile, _ = unit_rows(total)
        r.enc_v[pl.ds(at, tile), :] = low(unit_tile * vec(GAIN_FFN) + vec(SHIFT_FFN))
        spot = pl.ds(at, tile)
        pltpu.make_async_copy(r.enc_v.at[spot], r.encoded.at[spot], r.store_sem.at[0]).start()

    def sum_step(step):
        def act():
            sum_come(step - 1)
            sum_go(step)

        return act

    def stage_step(name, stage):
        return lambda: step_on(name, stage)

    def twin_spread():
        hold(r.a_recv.at[2], r.u_twin)
        spread(lambda rows: r.u_twin.at[rows], lambda slot: r.side_got.at[slot, 2], 5, 1, 1)

    def many_spread():
        for v in range(lanes // 128):
            r.t_side[v] = low(r.t_sum[128 * v : 128 * v + 128].T)
        spread_t(1, members)

    def few_spread():
        r.t_few[...] = few_rows(r.t_sum[...])
        spread(lambda rows: r.t_few.at[rows], lambda slot: r.few_got.at[slot], 1, 0, 0)

    QUERY_MOVES = {
        0: [stage_step(NORMED_ALL, 2), stage_step(X_ALL, 3)],
        2: [stage_step(BRANCH_ALL, 2), stage_step(NORMED_ALL, 3)],
        3: [sum_step(1), stage_step(FEW_ALL, 1), stage_step(QUERY_ALL, 2)],
        4: [sum_step(2), many_spread, stage_step(BRANCH_ALL, 3)],
        5: [few_turn, stage_step(FEW_ALL, 2)],
        6: [sum_step(3), stage_step(FEW_ALL, 3)],
        7: [sum_step(4)],
        8: [stage_step(QUERY_ALL, 3)],
    }
    PASSAGE_MOVES = {
        1: [stage_step(NORMED_ALL, 1), lambda: go(FEW_ALL, 1)],
        2: [sum_step(1), lambda: go(LAST_ALL, 1), stage_step(NORMED_ALL, 2)],
        3: [stage_step(ATTN_ALL, 1), stage_step(FEW_ALL, 2)],
        4: [sum_step(2), stage_step(MIXED_ALL, 2), stage_step(NORMED_ALL, 3)],
        5: [twin_spread, few_spread, stage_step(LAST_ALL, 2), stage_step(BRANCH_ALL, 2), stage_step(FEW_ALL, 3)],
        6: [stage_step(MIXED_ALL, 3)],
        7: [sum_step(3), stage_step(LAST_ALL, 3), stage_step(BRANCH_ALL, 3), stage_step(ATTN_ALL, 2)],
        8: [],
    }

    def moves(i, odd):
        for table, where in ((QUERY_MOVES, is_query), (PASSAGE_MOVES, is_passage)):
            for point, acts in table.items():
                if point // 2 < tiles and point % 2 == odd:

                    @pl.when(jnp.logical_and(i == point // 2, where))
                    def _():
                        for act in acts:
                            act()

    def turn(i, carry):
        attend_tile(i)

        @pl.when(jnp.logical_and(i == 0, is_query))
        def _():
            rank_rows()
            go(NORMED_ALL, 1)
            step_on(X_ALL, 2)

        @pl.when(jnp.logical_and(i == 1, is_passage))
        def _():
            passage_rows()
            step_on(BRANCH_ALL, 1)
            step_on(MIXED_ALL, 1)

        @pl.when(i == jnp.where(is_query, 0, 1))
        def _():
            backward_rows()

        moves(i, 0)
        feed_tile(i)
        moves(i, 1)
        return carry

    lax.fori_loop(0, tiles, turn, 0)

    for table, where in ((QUERY_MOVES, is_query), (PASSAGE_MOVES, is_passage)):

        @pl.when(where)
        def _():
            for act in table[2 * tiles]:
                act()


    def flatten(name, dst):
        rows_q = gathered[name][...].reshape(slots, 2 * cand, half)
        dst[0:query_rows, 0:half] = rows_q[:, 0:cand].reshape(query_rows, half)
        dst[0:query_rows, half:width] = rows_q[:, cand : 2 * cand].reshape(query_rows, half)
        when, at = divmod((TO_QUERY if name in TO_QUERY else TO_PASSAGE).index(name), 2)
        rows_p = r.few_all[when, :, :, :, PART * at : PART * at + PART].reshape(slots, PART, half)
        dst[query_rows:all_rows, :] = low(unpack_eight(rows_p))

    win = 256
    at48 = bat * share
    base48 = jnp.minimum(lax.div(at48, 128) * 128, width - win)
    off48 = pl.multiple_of(at48 - base48, 8)
    win48 = pl.ds(pl.multiple_of(base48, 128), win)
    share_in = hidden // members
    at192 = bat * share_in
    base192 = jnp.minimum(lax.div(at192, 128) * 128, hidden - win)
    off192 = pl.multiple_of(at192 - base192, 8)
    win192 = pl.ds(pl.multiple_of(base192, 128), win)
    mine48 = pl.ds(off48, share)
    side = hidden // 2
    own_side = pl.multiple_of(grp * side, 128)
    other_side = pl.multiple_of((1 - grp) * side, 128)

    def swap(at, src):
        remote(src, (r.swap_in0, r.swap_in1)[at], r.s_send.at[at], r.s_recv.at[at], (1 - grp, bat)).start()

    come(FEW_ALL, 3)
    few_come()
    come(NORMED_ALL, 3)
    flatten(NORMED_ALL, r.flat_a)
    come(BRANCH_ALL, 3)
    flatten(BRANCH_ALL, r.flat_b)
    step = side // 2

    def slope_cols(j, carry):
        span = pl.ds(pl.multiple_of(own_side + j * step, 128), step)
        slope_j = gelu_slope(nn(r.flat_a[...], r.w_in_v[:, span]) + r.b_in_v[:, span])
        pre_j = low(nt(r.flat_b[...], r.w_back_v[span, :]) * slope_j)
        here = pl.ds(pl.multiple_of(j * step, 128), step)
        r.stage[:, here] = tn(r.flat_a[:, win48], pre_j)
        return carry

    lax.fori_loop(0, 2, slope_cols, 0)
    piece = low(r.stage[mine48, :])
    r.swap_out0[...] = piece
    swap(0, r.swap_out0)
    r.g_in[:, pl.ds(own_side, side)] = wide(piece)
    @pl.when(is_passage)
    def _():
        sum_step(4)()
        step_on(ATTN_ALL, 3)

    active_win = low(gelu(nn(r.flat_a[...], r.w_in_v[:, win192]) + r.b_in_v[:, win192]))
    r.stage[:, 0:width] = tn(active_win, r.flat_b[...])
    r.g_back[...] = r.stage[pl.ds(off192, share_in), 0:width]

    def one_share(at, left, right):
        r.stage[:, 0:width] = tn(left[:, win48], right[...])
        r.swap_out1[at] = low(r.stage[mine48, 0:width])

    @pl.when(is_query)
    def _():
        come(X_ALL, 3)
        flatten(X_ALL, r.flat_c)
        come(QUERY_ALL, 3)
        flatten(QUERY_ALL, r.flat_d)
        one_share(0, r.flat_c, r.flat_d)
        r.factor[...] = (nn(r.flat_c[...], r.w_query_v[...]) + vec(B_QUERY)) * HD ** (-0.5)
        r.side_got[my_slot] = r.t_side[:, share_rows(bat)]
        hold(r.a_recv.at[0], r.side_got.at[pl.ds(0, members - 1)])
        hold(r.a_recv.at[1], r.few_got)

    @pl.when(is_passage)
    def _():
        come(MIXED_ALL, 3)
        flatten(MIXED_ALL, r.flat_c)
        come(ATTN_ALL, 3)
        flatten(ATTN_ALL, r.flat_d)
        one_share(0, r.flat_c, r.flat_d)
        r.factor[...] = nt(r.flat_d[...], r.w_out_v[...])
        r.side_got[my_slot, 2] = r.u_twin[share_rows(bat)]
        r.few_got[my_slot] = r.u_few[share_rows(bat)]
        hold(r.a_recv.at[4], r.side_got.at[:, pl.ds(0, 2)])
        hold(r.a_recv.at[5], r.side_got.at[pl.ds(0, members - 1), 2])
        hold(r.a_recv.at[3], r.few_got.at[pl.ds(0, members - 1)])

    head_4 = iota((1, HEADS_VREG, 1, HEADS_VREG * HD), 1)
    lane_4 = iota((1, HEADS_VREG, 1, HEADS_VREG * HD), 3) >> 6
    head_16 = iota((1, 16, 1, HEADS_VREG * HD), 1)
    lane_16 = iota((1, 16, 1, HEADS_VREG * HD), 3) >> 6
    few = jnp.concatenate([r.few_got[m] for m in range(slots)], axis=1)
    for v in range(H // HEADS_VREG):
        span = slice(256 * v, 256 * v + 256)
        left = jnp.concatenate([r.side_got[m, v] for m in range(slots)], axis=1)
        full = r.factor[0:query_rows, span].reshape(slots, 1, cand, 256)
        right = low(jnp.where(head_4 == lane_4, full, 0.0)).reshape(slots * 128, 256)
        total = nn(left, right)
        full = r.factor[query_rows:all_rows, span].reshape(slots, 1, 8, 256)
        right = low(jnp.where(head_16 == lane_16 + HEADS_VREG * v, full, 0.0)).reshape(slots * 128, 256)
        r.swap_out1[1, :, span] = low(total + nn(few, right))
    swap(1, r.swap_out1)

    @pl.when(is_query)
    def _():
        r.g_query[...] = wide(r.swap_out1[0])
        r.g_key[...] = wide(r.swap_out1[1])

    @pl.when(is_passage)
    def _():
        r.g_out[...] = wide(r.swap_out1[0])
        r.g_value[...] = wide(r.swap_out1[1])

    sum_come(4)
    mine = pltpu.roll(r.sum_out[5, 0:8], lax.rem(width - at48, width), 1)
    shares = (
        r.g_gain_ffn,
        r.g_shift_ffn,
        r.g_gain_attn,
        r.g_shift_attn,
        r.gb_query,
        r.gb_value,
        r.gb_out,
        r.gb_back,
    )
    for at, ref in enumerate(shares):
        ref[...] = mine[at : at + 1, 0:share].reshape(share)
    line = r.sum_out[5, pl.ds(8 + lax.div(at192, width), 1), :]
    line = pltpu.roll(
        jnp.broadcast_to(line, (8, width)), lax.rem(width - lax.rem(at192, width), width), 1
    )
    r.gb_in[...] = line[0:1, 0:share_in].reshape(share_in)

    hold(r.s_recv.at[0], r.swap_in0)
    r.g_in[:, pl.ds(other_side, side)] = wide(r.swap_in0[...])
    hold(r.s_recv.at[1], r.swap_in1)

    @pl.when(is_query)
    def _():
        r.g_out[...] = wide(r.swap_in1[0])
        r.g_value[...] = wide(r.swap_in1[1])

    @pl.when(is_passage)
    def _():
        r.g_query[...] = wide(r.swap_in1[0])
        r.g_key[...] = wide(r.swap_in1[1])

    hold(r.store_sem.at[0], r.enc_v)
    hold(r.store_sem.at[1], r.left)
    hold(r.store_sem.at[2], r.right)
    for name in range(len(gathered)):
        sent(name)
    few_sent()
    for at in range(5):
        hold(r.v_send.at[at], r.sum_out.at[at])
    hold(r.s_send.at[0], r.swap_out0)
    hold(r.s_send.at[1], r.swap_out1)

    @pl.when(is_query)
    def _():
        hold(r.a_send.at[0], r.side_got.at[pl.ds(0, members - 1)])
        hold(r.a_send.at[2], r.u_twin)
        hold(r.a_send.at[4], r.side_got.at[:, pl.ds(0, 2)])
        hold(r.b_send.at[1], r.pas_in.at[core])
        hold(r.b_send.at[2], r.pas_twin)
        hold(r.b_send.at[3], r.pas_sum)

    @pl.when(is_passage)
    def _():
        hold(r.a_send.at[1], r.few_got)
        hold(r.a_send.at[3], r.few_got.at[pl.ds(0, members - 1)])
        hold(r.a_send.at[5], r.side_got.at[pl.ds(0, members - 1), 2])
        hold(r.b_send.at[0], r.pas_got)


def result_kernel(count, *refs):
    ins, outs = refs[: count + 1], refs[count + 1 : 2 * count + 1]
    held, (tile_out, load_sem, store_sem, grad_sem) = refs[2 * count + 1 : -4], refs[-4:]
    loads = [pltpu.make_async_copy(src, dst, load_sem.at[at]) for at, (src, dst) in enumerate(zip(ins, held))]
    for at in (1, 2, 0) + tuple(range(3, count + 1)):
        loads[at].start()
    places = (0,) + tuple(range(2, count))
    stores = [
        pltpu.make_async_copy(held[at + 1 if at else 0], outs[at], store_sem.at[at]) for at in places
    ]
    loads[1].wait()
    loads[2].wait()
    tile = tile_out.shape[0] // 4
    grads = []
    for i in range(4):
        spot = slice(i * tile, (i + 1) * tile)
        tile_out[spot, :] = tn(held[1][:, spot], held[2][...])
        grads.append(pltpu.make_async_copy(tile_out.at[spot], outs[1].at[spot], grad_sem.at[i]))
        grads[-1].start()
        if i == 0:
            for at, store in zip(places, stores):
                loads[at + 1 if at else 0].wait()
                store.start()
    for copy in grads + stores:
        copy.wait()


def make_shards(groups, members):
    def shards(*args):
        tokens = args[0]
        rows, width = tokens.shape
        hidden = Ins(*args).w_in.shape[1]
        share, share_in = width // members, hidden // members
        cand = rows // QLEN
        lanes = H * cand
        all_rows = members * (cand + 8)
        per_core = (groups - 1) * members // 2
        across = members // 8
        half = width // 2
        f32, bf16 = jnp.float32, jnp.bfloat16
        out_shapes = Outs(
            encoded=((rows, width), bf16),
            left_out=((2 * lanes + 2 * cand, rows), bf16),
            right_out=((2 * lanes + 2 * cand, width), bf16),
            g_query=((share, width), f32),
            gb_query=((share,), f32),
            g_key=((share, width), f32),
            g_value=((share, width), f32),
            gb_value=((share,), f32),
            g_out=((share, width), f32),
            gb_out=((share,), f32),
            g_gain_attn=((share,), f32),
            g_shift_attn=((share,), f32),
            g_in=((share, hidden), f32),
            gb_in=((share_in,), f32),
            g_back=((share_in, width), f32),
            gb_back=((share,), f32),
            g_gain_ffn=((share,), f32),
            g_shift_ffn=((share,), f32),
        )
        out_shape = tuple(jax.ShapeDtypeStruct(*pair) for pair in out_shapes)
        dma = pltpu.SemaphoreType.DMA
        gathered = pltpu.VMEM((2, across, 4, 2 * cand, half), bf16)
        scratch = Scratch(
            tokens_v=pltpu.VMEM((rows, width), bf16),
            w_query_v=pltpu.VMEM((width, width), bf16),
            w_key_v=pltpu.VMEM((width, width), bf16),
            w_value_v=pltpu.VMEM((width, width), bf16),
            w_out_v=pltpu.VMEM((width, width), bf16),
            w_in_v=pltpu.VMEM((width, hidden), bf16),
            w_back_v=pltpu.VMEM((hidden, width), bf16),
            vectors_v=pltpu.VMEM((8, width), f32),
            b_in_1d=pltpu.VMEM((hidden,), f32),
            vector_sem=dma((9,)),
            rows_v=pltpu.VMEM((8, width), f32),
            t_sum=pltpu.VMEM((lanes, width), f32),
            b_in_v=pltpu.VMEM((1, hidden), f32),
            key_seg=pltpu.VMEM((rows // 256, 1, 256), jnp.int32),
            left=pltpu.VMEM((2 * lanes + 2 * cand, rows), bf16),
            right=pltpu.VMEM((2 * lanes + 2 * cand, width), bf16),
            prob=pltpu.VMEM((lanes, rows), f32),
            slope=pltpu.VMEM((cand, hidden), f32),
            unit_one=pltpu.VMEM((cand, width), f32),
            rate_one=pltpu.VMEM((cand, 1), f32),
            unit_two=pltpu.VMEM((cand, width), f32),
            rate_two=pltpu.VMEM((cand, 1), f32),
            cls=pltpu.VMEM((cand, width), bf16),
            y_grad=pltpu.VMEM((cand, width), f32),
            x_all=gathered,
            mixed_all=gathered,
            normed_all=gathered,
            branch_all=gathered,
            attn_all=gathered,
            query_all=gathered,
            few_all=pltpu.VMEM((2, 2, across, 4, 2 * PART, half), bf16),
            few_out=pltpu.VMEM((2, 2 * PART, half), bf16),
            t_side=pltpu.VMEM((lanes // 128, width, 128), bf16),
            u_side=pltpu.VMEM((lanes // 128, width, 128), bf16),
            u_twin=pltpu.VMEM((width, 128), bf16),
            t_few=pltpu.VMEM((width, 128), bf16),
            u_few=pltpu.VMEM((width, 128), bf16),
            side_got=pltpu.VMEM((members, lanes // 128, share, 128), bf16),
            few_got=pltpu.VMEM((members, share, 128), bf16),
            sum_out=pltpu.VMEM((6, 16, width), f32),
            sum_in=pltpu.VMEM((5, 16, width), f32),
            pas_out=pltpu.VMEM((PART, half), bf16),
            pas_in=pltpu.VMEM((2, per_core, PART, half), bf16),
            pas_part=pltpu.VMEM((2, per_core, PART, half), bf16),
            pas_twin=pltpu.VMEM((per_core, PART, half), bf16),
            pas_sum=pltpu.VMEM((per_core, PART, half), bf16),
            pas_got=pltpu.VMEM((members // 2, PART, half), bf16),
            normed_v=pltpu.VMEM((256, width), f32),
            enc_v=pltpu.VMEM((rows, width), bf16),
            flat_a=pltpu.VMEM((all_rows, width), bf16),
            flat_b=pltpu.VMEM((all_rows, width), bf16),
            flat_c=pltpu.VMEM((all_rows, width), bf16),
            flat_d=pltpu.VMEM((all_rows, width), bf16),
            factor=pltpu.VMEM((all_rows, width), f32),
            stage=pltpu.VMEM((256, hidden // 2), f32),
            swap_out0=pltpu.VMEM((share, hidden // 2), bf16),
            swap_in0=pltpu.VMEM((share, hidden // 2), bf16),
            swap_out1=pltpu.VMEM((2, share, width), bf16),
            swap_in1=pltpu.VMEM((2, share, width), bf16),
            load_sem=dma((7,)),
            store_sem=dma((3,)),
            g_send=dma((8, 4)),
            g_recv=dma((8, 4)),
            f_send=dma((2,)),
            f_recv=dma((2,)),
            v_send=dma((5,)),
            v_recv=dma((5,)),
            a_send=dma((6,)),
            a_recv=dma((6,)),
            b_send=dma((4,)),
            b_recv=dma((4,)),
            s_send=dma((2,)),
            s_recv=dma((2,)),
        )
        anywhere = pl.BlockSpec(memory_space=pl.ANY)
        vmem = pl.BlockSpec(memory_space=pltpu.VMEM)
        smem = pl.BlockSpec(memory_space=pltpu.SMEM)
        in_specs = [anywhere] * len(args)
        for at in range(1, 4):
            in_specs[at] = smem
        out_specs = (anywhere,) * 3 + (vmem,) * (len(out_shape) - 3)
        made = pl.pallas_call(
            functools.partial(main_kernel, (groups, members, rows, width, hidden)),
            out_shape=out_shape,
            in_specs=in_specs,
            out_specs=out_specs,
            scratch_shapes=list(scratch),
            name="layer",
            compiler_params=pltpu.CompilerParams(
                collective_id=0, has_side_effects=True, vmem_limit_bytes=60 * 1024 * 1024
            ),
        )(*args)
        results = (out_shape[0], jax.ShapeDtypeStruct((rows, width), f32)) + out_shape[3:]
        count = len(results)
        return pl.pallas_call(
            functools.partial(result_kernel, count),
            out_shape=results,
            in_specs=[anywhere] * (count + 1),
            out_specs=(anywhere,) * count,
            scratch_shapes=[pltpu.VMEM(shape.shape, shape.dtype) for shape in out_shape]
            + [pltpu.VMEM((rows, width), f32), dma((count + 1,)), dma((count,)), dma((4,))],
            name="results",
            compiler_params=pltpu.CompilerParams(vmem_limit_bytes=60 * 1024 * 1024),
        )(*made)

    return shards


def solution(mesh):
    in_specs = (
        P(("grp", "batch"), None),
        P(("grp", "batch")),
        P(("grp", "batch"), None),
        P(),
        P(),
        P(),
        P(),
        P(),
        P(),
        P(),
        P(),
        P(),
        P(),
        P(),
        P(),
        P(),
        P(),
        P(),
        P(),
    )
    out_specs = (
        P(("grp", "batch"), None),
        P(("grp", "batch"), None),
        P("batch", None),
        P("batch"),
        P("batch", None),
        P("batch", None),
        P("batch"),
        P("batch", None),
        P("batch"),
        P("batch"),
        P("batch"),
        P("batch", None),
        P("batch"),
        P("batch", None),
        P("batch"),
        P("batch"),
        P("batch"),
    )
    groups, members = mesh.shape["grp"], mesh.shape["batch"]
    fits = groups == 2 and members == 16
    shards = make_shards(groups, members) if fits else plain_shards
    return jax.shard_map(shards, mesh=mesh, in_specs=in_specs, out_specs=out_specs, check_vma=False)
```

```python
import functools
import typing

import jax
import jax.numpy as jnp
from jax import lax
from jax.experimental import pallas as pl
from jax.experimental.pallas import tpu as pltpu
from jax.sharding import PartitionSpec as P

H = 12
HD = 64
QLEN = 32
SHORT = 128
LONG = 256
BLK = 512
SLOTS_BLK = 16
PAS_DEV = 6


norm_epsilon = 1e-06


def matmul(left, right):
    return jnp.dot(left, right, preferred_element_type=jnp.float32)


def matmul_tn(left, right):
    return lax.dot_general(
        left, right, (((0,), (0,)), ((), ())), preferred_element_type=jnp.float32
    )


def matmul_nt(left, right):
    return lax.dot_general(
        left, right, (((1,), (1,)), ((), ())), preferred_element_type=jnp.float32
    )


def gelu_exact(values):
    return jax.nn.gelu(values, approximate=False)


def slot_sizes(buckets):
    return jnp.where(buckets == 0, QLEN, jnp.where(buckets == 1, SHORT, LONG)).astype(jnp.int32)


def candidates(buckets):
    sizes_here = slot_sizes(buckets)
    slot_index = jnp.arange(SLOTS_BLK, dtype=jnp.int32)
    starts = slot_index[None, :] * sizes_here[:, None]
    inside = starts < BLK
    return (jnp.where(inside, starts, 0), inside)


def compact_order(inside):
    flattened = inside.reshape(-1)
    places = jnp.arange(flattened.shape[0], dtype=jnp.int32)
    return jnp.argsort(jnp.where(flattened, places, places + flattened.shape[0]))


def block_mask(bucket, slot_lengths):
    width_slot = slot_sizes(bucket)
    places = jnp.arange(BLK, dtype=jnp.int32)
    segment = places // width_slot
    within = places - segment * width_slot
    slot_index = jnp.arange(SLOTS_BLK, dtype=jnp.int32)
    limits = jnp.sum(
        jnp.where(segment[:, None] == slot_index[None, :], slot_lengths[None, :], 0), axis=1
    )
    return (segment[:, None] == segment[None, :]) & (within < limits)[None, :]


def layer_norm(hidden, scale_vec, shift_vec):
    center = hidden - jnp.mean(hidden, axis=-1, keepdims=True)
    spread = jnp.mean(center * center, axis=-1, keepdims=True)
    return center * lax.rsqrt(spread + norm_epsilon) * scale_vec + shift_vec


def rank_gradient(query_block, passages, picked, score_scale):
    scores = matmul_nt(query_block, passages) * score_scale
    targets = (jnp.arange(passages.shape[0], dtype=jnp.int32)[None, :] == picked[:, None]).astype(
        jnp.float32
    )
    return (jax.nn.softmax(scores, axis=1) - targets).astype(jnp.bfloat16)


def plain_shards(
    tokens,
    buckets,
    lengths,
    positives,
    w_query,
    b_query,
    w_key,
    w_value,
    b_value,
    w_out,
    b_out,
    gain_attn,
    shift_attn,
    w_in,
    b_in,
    w_back,
    b_back,
    gain_ffn,
    shift_ffn,
):
    tok_rows = tokens.shape[0]
    width = tokens.shape[1]
    blocks = tok_rows // BLK
    block_shape = (blocks, BLK, H, HD)
    head_scale = HD ** (-0.5)
    inputs = tokens.astype(jnp.float32)
    query_rows = (matmul(tokens, w_query) + b_query).astype(jnp.bfloat16)
    key_rows = matmul(tokens, w_key).astype(jnp.bfloat16)
    value_rows = (matmul(tokens, w_value) + b_value).astype(jnp.bfloat16)

    def attend(packed):
        query_blk, key_blk, value_blk, bucket, slot_lengths = packed
        scores = (
            jnp.einsum("qhd,khd->hqk", query_blk, key_blk, preferred_element_type=jnp.float32)
            * head_scale
        )
        scores = jnp.where(block_mask(bucket, slot_lengths)[None], scores, -1e30)
        highest = jnp.max(scores, axis=-1, keepdims=True)
        raised = jnp.exp(scores - highest)
        row_totals = jnp.sum(raised, axis=-1, keepdims=True)
        weights = (raised / row_totals).astype(jnp.bfloat16)
        mixed_blk = jnp.einsum(
            "hqk,khd->qhd", weights, value_blk, preferred_element_type=jnp.float32
        )
        return (mixed_blk.astype(jnp.bfloat16), (highest + jnp.log(row_totals))[..., 0])

    mixed_heads, log_totals = lax.map(
        attend,
        (
            query_rows.reshape(block_shape),
            key_rows.reshape(block_shape),
            value_rows.reshape(block_shape),
            buckets,
            lengths,
        ),
    )
    mixed_heads = mixed_heads.reshape(tok_rows, width)
    hidden_one = inputs + matmul(mixed_heads, w_out) + b_out
    normed = layer_norm(hidden_one, gain_attn, shift_attn)
    normed_low = normed.astype(jnp.bfloat16)
    hidden_pre = matmul(normed_low, w_in) + b_in
    active = gelu_exact(hidden_pre).astype(jnp.bfloat16)
    hidden_two = normed + matmul(active, w_back) + b_back
    output = layer_norm(hidden_two, gain_ffn, shift_ffn)
    encoded = output.astype(jnp.bfloat16)
    slot_starts, inside = candidates(buckets)
    cand_rows = (slot_starts + BLK * jnp.arange(blocks, dtype=jnp.int32)[:, None]).reshape(-1)
    order_index = compact_order(inside)
    inverse_index = jnp.argsort(order_index)
    cls_count = cand_rows.shape[0]
    cls_mine = output[cand_rows[order_index]].astype(jnp.bfloat16)
    groups = lax.axis_size("grp")
    members = lax.axis_size("batch")
    group_here = lax.axis_index("grp")
    member_here = lax.axis_index("batch")
    gathered = lax.all_gather(cls_mine, ("grp", "batch"), axis=0, tiled=True).reshape(
        groups, members, cls_count, width
    )
    queries = gathered[0].reshape(members * cls_count, width)
    passages = gathered[1:, :, :PAS_DEV].reshape((groups - 1) * members * PAS_DEV, width)
    score_scale = width ** (-0.5)
    query_share = cls_count // groups
    first_query = member_here * cls_count + group_here * query_share
    own_queries = lax.dynamic_slice_in_dim(queries, first_query, query_share, 0)
    own_picked = lax.dynamic_slice_in_dim(positives, first_query, query_share, 0)
    rank_grad = rank_gradient(own_queries, passages, own_picked, score_scale)
    query_part = matmul(rank_grad, passages) * score_scale
    query_rows_grad = lax.all_gather(query_part, "grp", axis=0, tiled=True)
    passage_terms = jnp.concatenate(
        [
            jnp.zeros((members * PAS_DEV, width), jnp.float32),
            matmul_tn(rank_grad, own_queries) * score_scale,
        ],
        axis=0,
    )
    passage_rows_grad = lax.psum_scatter(
        passage_terms, ("grp", "batch"), scatter_dimension=0, tiled=True
    )
    padded_passage = jnp.pad(passage_rows_grad, ((0, cls_count - PAS_DEV), (0, 0)))
    cls_grad = jnp.where(group_here == 0, query_rows_grad, padded_passage)
    output_grad = cls_grad[inverse_index]
    kept_two, pull_two = jax.vjp(layer_norm, hidden_two[cand_rows], gain_ffn, shift_ffn)
    two_grad, gain_ffn_grad, shift_ffn_grad = pull_two(output_grad)
    branch_grad = two_grad.astype(jnp.bfloat16)
    b_back_grad = jnp.sum(branch_grad.astype(jnp.float32), axis=0)
    w_back_grad = matmul_tn(active[cand_rows], branch_grad)
    kept_gelu, pull_gelu = jax.vjp(gelu_exact, hidden_pre[cand_rows])
    pre_grad = pull_gelu(matmul_nt(branch_grad, w_back))[0].astype(jnp.bfloat16)
    b_in_grad = jnp.sum(pre_grad.astype(jnp.float32), axis=0)
    w_in_grad = matmul_tn(normed_low[cand_rows], pre_grad)
    normed_grad = two_grad + matmul_nt(pre_grad, w_in)
    kept_one, pull_one = jax.vjp(layer_norm, hidden_one[cand_rows], gain_attn, shift_attn)
    one_grad, gain_attn_grad, shift_attn_grad = pull_one(normed_grad)
    attn_grad = one_grad.astype(jnp.bfloat16)
    b_out_grad = jnp.sum(attn_grad.astype(jnp.float32), axis=0)
    w_out_grad = matmul_tn(mixed_heads[cand_rows], attn_grad)
    mixed_grad = matmul_nt(attn_grad, w_out).astype(jnp.bfloat16)
    slots_block = slot_starts.shape[1]
    row_shape = (blocks, slots_block, H, HD)
    query_cls = query_rows[cand_rows].reshape(row_shape)
    mixed_cls = mixed_grad.reshape(row_shape)
    log_cls = jnp.take_along_axis(
        log_totals, jnp.broadcast_to(slot_starts[:, None, :], (blocks, H, slots_block)), axis=2
    )

    def attend_back(packed):
        query_blk, key_blk, value_blk, grad_blk, log_blk, bucket, slot_lengths, start_blk = packed
        visible = block_mask(bucket, slot_lengths)[start_blk]
        scores_blk = (
            jnp.einsum("shd,khd->hsk", query_blk, key_blk, preferred_element_type=jnp.float32)
            * head_scale
        )
        scores_blk = jnp.where(visible[None], scores_blk, -1e30)
        weights = jnp.exp(scores_blk - log_blk[..., None])
        value_back = jnp.einsum(
            "hsk,shd->khd",
            weights.astype(jnp.bfloat16),
            grad_blk,
            preferred_element_type=jnp.float32,
        )
        weight_grad = jnp.einsum(
            "shd,khd->hsk", grad_blk, value_blk, preferred_element_type=jnp.float32
        )
        score_back = (
            weights * (weight_grad - jnp.sum(weights * weight_grad, axis=-1, keepdims=True))
        ).astype(jnp.bfloat16)
        query_back = (
            jnp.einsum("hsk,khd->shd", score_back, key_blk, preferred_element_type=jnp.float32)
            * head_scale
        )
        key_back = (
            jnp.einsum("hsk,shd->khd", score_back, query_blk, preferred_element_type=jnp.float32)
            * head_scale
        )
        return (query_back, key_back, value_back)

    query_back, key_back, value_back = lax.map(
        attend_back,
        (
            query_cls,
            key_rows.reshape(block_shape),
            value_rows.reshape(block_shape),
            mixed_cls,
            log_cls,
            buckets,
            lengths,
            slot_starts,
        ),
    )
    query_back = query_back.reshape(cls_count, width).astype(jnp.bfloat16)
    key_back = key_back.reshape(tok_rows, width).astype(jnp.bfloat16)
    value_back = value_back.reshape(tok_rows, width).astype(jnp.bfloat16)
    b_query_grad = jnp.sum(query_back.astype(jnp.float32), axis=0)
    w_query_grad = matmul_tn(tokens[cand_rows], query_back)
    w_key_grad = matmul_tn(tokens, key_back)
    w_value_grad = matmul_tn(tokens, value_back)
    b_value_grad = jnp.sum(value_back.astype(jnp.float32), axis=0)
    row_grad = one_grad + matmul_nt(query_back, w_query)
    tokens_grad = (
        (matmul_nt(key_back, w_key) + matmul_nt(value_back, w_value)).at[cand_rows].add(row_grad)
    )
    all_shares = (
        lax.psum_scatter(w_query_grad, "batch", scatter_dimension=0, tiled=True),
        lax.psum_scatter(b_query_grad, "batch", scatter_dimension=0, tiled=True),
        lax.psum_scatter(w_key_grad, "batch", scatter_dimension=0, tiled=True),
        lax.psum_scatter(w_value_grad, "batch", scatter_dimension=0, tiled=True),
        lax.psum_scatter(b_value_grad, "batch", scatter_dimension=0, tiled=True),
        lax.psum_scatter(w_out_grad, "batch", scatter_dimension=0, tiled=True),
        lax.psum_scatter(b_out_grad, "batch", scatter_dimension=0, tiled=True),
        lax.psum_scatter(gain_attn_grad, "batch", scatter_dimension=0, tiled=True),
        lax.psum_scatter(shift_attn_grad, "batch", scatter_dimension=0, tiled=True),
        lax.psum_scatter(w_in_grad, "batch", scatter_dimension=0, tiled=True),
        lax.psum_scatter(b_in_grad, "batch", scatter_dimension=0, tiled=True),
        lax.psum_scatter(w_back_grad, "batch", scatter_dimension=0, tiled=True),
        lax.psum_scatter(b_back_grad, "batch", scatter_dimension=0, tiled=True),
        lax.psum_scatter(gain_ffn_grad, "batch", scatter_dimension=0, tiled=True),
        lax.psum_scatter(shift_ffn_grad, "batch", scatter_dimension=0, tiled=True),
    )
    summed = tuple(
        lax.psum(
            (
                all_shares[0],
                all_shares[1],
                all_shares[2],
                all_shares[3],
                all_shares[4],
                all_shares[5],
                all_shares[6],
                all_shares[7],
                all_shares[8],
                all_shares[9],
                all_shares[10],
                all_shares[11],
                all_shares[12],
                all_shares[13],
                all_shares[14],
            ),
            "grp",
        )
    )
    return (
        encoded,
        tokens_grad,
        summed[0],
        summed[1],
        summed[2],
        summed[3],
        summed[4],
        summed[5],
        summed[6],
        summed[7],
        summed[8],
        summed[9],
        summed[10],
        summed[11],
        summed[12],
        summed[13],
        summed[14],
    )


MESH = pl.DeviceIdType.MESH
HEADS_VREG = 4
PART = 16


def nn(left, right):
    return lax.dot_general(
        left, right, (((1,), (0,)), ((), ())), preferred_element_type=jnp.float32
    )


def nt(left, right):
    return lax.dot_general(
        left, right, (((1,), (1,)), ((), ())), preferred_element_type=jnp.float32
    )


def tn(left, right):
    return lax.dot_general(
        left, right, (((0,), (0,)), ((), ())), preferred_element_type=jnp.float32
    )


def low(values):
    return values.astype(jnp.bfloat16)


def wide(values):
    return values.astype(jnp.float32)


def iota(shape, axis):
    return lax.broadcasted_iota(jnp.int32, shape, axis)


def gelu(values):
    middle = 0.5 * values
    return middle + middle * lax.erf(values * 0.7071067811865476)


def gelu_slope(values):
    below = 0.5 + 0.5 * lax.erf(values * 0.7071067811865476)
    return below + values * (0.3989422804014327 * jnp.exp(-0.5 * (values * values)))


def gelu_both(values):
    below = 0.5 + 0.5 * lax.erf(values * 0.7071067811865476)
    bell = 0.3989422804014327 * jnp.exp(-0.5 * (values * values))
    return values * below, below + values * bell


def unit_rows(hidden):
    center = hidden - jnp.mean(hidden, axis=-1, keepdims=True)
    rate = lax.rsqrt(jnp.mean(center * center, axis=-1, keepdims=True) + norm_epsilon)
    return center * rate, rate


def norm_back(grad, unit, rate, gain):
    scaled = grad * gain
    return rate * (
        scaled
        - jnp.mean(scaled, axis=-1, keepdims=True)
        - unit * jnp.mean(scaled * unit, axis=-1, keepdims=True)
    )


def hold(sem, ref):
    pltpu.make_async_copy(ref, ref, sem).wait()


def pack_eight(values):
    middle = values.shape[1] // 2
    values = wide(values)
    return low(jnp.concatenate([values[:, :middle], values[:, middle:]], axis=0))


def unpack_eight(values):
    count, _, middle = values.shape
    values = wide(values)
    return jnp.concatenate(
        [values[:, 0:8].reshape(8 * count, middle), values[:, 8:16].reshape(8 * count, middle)], axis=1
    )


class Ins(typing.NamedTuple):
    tokens: typing.Any
    buckets: typing.Any
    lengths: typing.Any
    positives: typing.Any
    w_query: typing.Any
    b_query: typing.Any
    w_key: typing.Any
    w_value: typing.Any
    b_value: typing.Any
    w_out: typing.Any
    b_out: typing.Any
    gain_attn: typing.Any
    shift_attn: typing.Any
    w_in: typing.Any
    b_in: typing.Any
    w_back: typing.Any
    b_back: typing.Any
    gain_ffn: typing.Any
    shift_ffn: typing.Any


class Outs(typing.NamedTuple):
    encoded: typing.Any
    left_out: typing.Any
    right_out: typing.Any
    g_query: typing.Any
    gb_query: typing.Any
    g_key: typing.Any
    g_value: typing.Any
    gb_value: typing.Any
    g_out: typing.Any
    gb_out: typing.Any
    g_gain_attn: typing.Any
    g_shift_attn: typing.Any
    g_in: typing.Any
    gb_in: typing.Any
    g_back: typing.Any
    gb_back: typing.Any
    g_gain_ffn: typing.Any
    g_shift_ffn: typing.Any


class Scratch(typing.NamedTuple):
    tokens_v: typing.Any
    w_query_v: typing.Any
    w_key_v: typing.Any
    w_value_v: typing.Any
    w_out_v: typing.Any
    w_in_v: typing.Any
    w_back_v: typing.Any
    vectors_v: typing.Any
    b_in_1d: typing.Any
    vector_sem: typing.Any
    rows_v: typing.Any
    t_sum: typing.Any
    b_in_v: typing.Any
    key_seg: typing.Any
    left: typing.Any
    right: typing.Any
    prob: typing.Any
    slope: typing.Any
    unit_one: typing.Any
    rate_one: typing.Any
    unit_two: typing.Any
    rate_two: typing.Any
    cls: typing.Any
    y_grad: typing.Any
    x_all: typing.Any
    mixed_all: typing.Any
    normed_all: typing.Any
    branch_all: typing.Any
    attn_all: typing.Any
    query_all: typing.Any
    few_all: typing.Any
    few_out: typing.Any
    t_side: typing.Any
    u_side: typing.Any
    u_twin: typing.Any
    t_few: typing.Any
    u_few: typing.Any
    side_got: typing.Any
    t_twin: typing.Any
    sum_out: typing.Any
    sum_in: typing.Any
    pas_out: typing.Any
    pas_in: typing.Any
    pas_part: typing.Any
    pas_twin: typing.Any
    pas_sum: typing.Any
    pas_got: typing.Any
    normed_v: typing.Any
    enc_v: typing.Any
    flat_a: typing.Any
    flat_b: typing.Any
    flat_c: typing.Any
    flat_d: typing.Any
    factor: typing.Any
    stage: typing.Any
    swap_out0: typing.Any
    swap_in0: typing.Any
    swap_out1: typing.Any
    swap_in1: typing.Any
    load_sem: typing.Any
    store_sem: typing.Any
    g_send: typing.Any
    g_recv: typing.Any
    f_send: typing.Any
    f_recv: typing.Any
    v_send: typing.Any
    v_recv: typing.Any
    a_send: typing.Any
    a_recv: typing.Any
    b_send: typing.Any
    b_recv: typing.Any
    s_send: typing.Any
    s_recv: typing.Any


class Refs:
    pass


X_ALL, MIXED_ALL, NORMED_ALL, BRANCH_ALL, ATTN_ALL, QUERY_ALL, FEW_ALL, LAST_ALL = range(8)
TO_QUERY = (X_ALL, NORMED_ALL, BRANCH_ALL, QUERY_ALL)
TO_PASSAGE = (MIXED_ALL, NORMED_ALL, BRANCH_ALL, ATTN_ALL)
EARLY, LATE = range(2)
B_QUERY, B_VALUE, B_OUT, GAIN_ATTN, SHIFT_ATTN, B_BACK, GAIN_FFN, SHIFT_FFN = range(8)
W_QUERY, W_KEY, W_VALUE, W_OUT, W_IN, W_BACK, TOKENS = range(7)


def main_kernel(sizes, *refs):
    groups, members, rows, width, hidden = sizes
    r = Refs()
    ends = (len(Ins._fields), len(Ins._fields) + len(Outs._fields))
    for group in (Ins(*refs[: ends[0]]), Outs(*refs[ends[0] : ends[1]]), Scratch(*refs[ends[1] :])):
        r.__dict__.update(group._asdict())
    across = members // 8
    depth = 4
    share = width // members
    cand = rows // QLEN
    lanes = H * cand
    slots = members
    query_rows = slots * cand
    all_rows = query_rows + slots * 8
    half = width // 2
    score_scale = width ** (-0.5)

    grp = lax.axis_index("grp")
    bat = lax.axis_index("batch")
    core = lax.rem(bat, 2)
    col = lax.rem(lax.div(bat, 2), across)
    lay = lax.div(bat, 2 * across)
    sibling = bat + 1 - 2 * core
    is_query = grp == 0
    is_passage = grp > 0

    def slot_of(member):
        return (
            lax.rem(member, 2) * across + lax.rem(lax.div(member, 2), across)
        ) * depth + lax.div(member, 2 * across)

    my_slot = slot_of(bat)

    weights = (r.w_query, r.w_key, r.w_value, r.w_out, r.w_in, r.w_back, r.tokens)
    held = (r.w_query_v, r.w_key_v, r.w_value_v, r.w_out_v, r.w_in_v, r.w_back_v, r.tokens_v)

    def load(at):
        return pltpu.make_async_copy(weights[at], held[at], r.load_sem.at[at])

    load(TOKENS).start()

    vectors = (
        r.b_query,
        r.b_value,
        r.b_out,
        r.gain_attn,
        r.shift_attn,
        r.b_back,
        r.gain_ffn,
        r.shift_ffn,
    )
    vector_loads = [
        pltpu.make_async_copy(vector, r.vectors_v.at[at], r.vector_sem.at[at]) for at, vector in enumerate(vectors)
    ]
    vector_loads.append(pltpu.make_async_copy(r.b_in, r.b_in_1d, r.vector_sem.at[len(vectors)]))
    for copy in vector_loads:
        copy.start()
    for at in (W_QUERY, W_KEY):
        load(at).start()

    barrier = pltpu.get_barrier_semaphore()

    def greet(step, carry):
        other = lax.rem(bat + step, members)

        @pl.when(step > 0)
        def _():
            pl.semaphore_signal(barrier, inc=1, device_id=(grp, other), device_id_type=MESH)

        pl.semaphore_signal(barrier, inc=1, device_id=(1 - grp, other), device_id_type=MESH)
        return carry

    lax.fori_loop(0, members, greet, 0)

    def remote(src, dst, send, recv, to):
        return pltpu.make_async_remote_copy(
            src_ref=src, dst_ref=dst, send_sem=send, recv_sem=recv, device_id=to, device_id_type=MESH
        )

    def vec(at):
        return r.rows_v[at : at + 1, :]

    def bucket_of(block):
        return r.buckets[block]

    def size_of(bucket):
        return jnp.where(bucket == 0, QLEN, jnp.where(bucket == 1, SHORT, LONG))

    def count_of(bucket):
        return jnp.where(bucket == 0, BLK // QLEN, jnp.where(bucket == 1, BLK // SHORT, BLK // LONG))

    first, second = bucket_of(0), bucket_of(1)
    first_count, second_count = count_of(first), count_of(second)

    def listed(index):
        later = index - first_count
        inside = index < first_count + second_count
        place = jnp.where(index < first_count, index * size_of(first), BLK + later * size_of(second))
        segment = jnp.where(index < first_count, index, SLOTS_BLK + later)
        return jnp.where(inside, place, -1), jnp.where(inside, segment, -2)

    def segment_of(token, bucket):
        within = token & (BLK - 1)
        slot = jnp.where(
            bucket == 0, within >> 5, jnp.where(bucket == 1, within >> 7, within >> 8)
        )
        place = jnp.where(
            bucket == 0, within & (QLEN - 1), jnp.where(bucket == 1, within & (SHORT - 1), within & (LONG - 1))
        )
        return slot + SLOTS_BLK * (token >> 9), place

    token = iota((1, rows), 1)
    bucket_row = jnp.where(token < BLK, first, second)
    segment_row, place_row = segment_of(token, bucket_row)
    limit_row = jnp.zeros((1, rows), jnp.int32)
    for at in range(rows // BLK * SLOTS_BLK):
        used = r.lengths[at // SLOTS_BLK, at % SLOTS_BLK]
        limit_row = jnp.where(segment_row == at, used, limit_row)
    key_segment = jnp.where(place_row < limit_row, segment_row, -1)
    for at in range(rows // 256):
        r.key_seg[at] = key_segment[:, 256 * at : 256 * at + 256]

    lane_head = iota((cand, width), 1) >> 6

    def by_head(values):
        values = wide(values)
        return low(
            jnp.concatenate([jnp.where(lane_head == h, values, 0.0) for h in range(H)], axis=0)
        )

    def pick_heads(values):
        total = jnp.zeros((cand, width), jnp.float32)
        for h in range(H):
            total = total + jnp.where(lane_head == h, values[h * cand : (h + 1) * cand], 0.0)
        return total

    gathered = (r.x_all, r.mixed_all, r.normed_all, r.branch_all, r.attn_all, r.query_all, r.few_all.at[EARLY], r.few_all.at[LATE])

    def keep(name, values):
        @pl.when(is_query)
        def _():
            gathered[name][core, col, lay, 0:cand] = values[:, :half]
            gathered[name][core, col, lay, cand : 2 * cand] = values[:, half:]

        @pl.when(is_passage)
        def _():
            packed = pack_eight(values[0:8])
            if name in TO_QUERY:
                when, at = divmod(TO_QUERY.index(name), 2)
                r.few_out[when, PART * at : PART * at + PART] = packed
            if name in TO_PASSAGE:
                when, at = divmod(TO_PASSAGE.index(name), 2)
                r.few_all[when, core, col, lay, PART * at : PART * at + PART] = packed

    def few_rows(values):
        eight = values.reshape(H, cand, width)[:, 0:8].reshape(8 * H, width)
        return low(jnp.concatenate([eight, jnp.zeros((128 - 8 * H, width), jnp.float32)], axis=0).T)

    def goes_to(name):
        if name == FEW_ALL or name in TO_QUERY and name in TO_PASSAGE:
            return grp >= 0
        return is_query if name in TO_QUERY else is_passage

    def sems(name, stage):
        return r.g_send.at[name, stage], r.g_recv.at[name, stage]

    def my_piece(name):
        return gathered[name].at[core, col, lay]

    def go(name, stage):
        buf = gathered[name]
        send, recv = sems(name, stage)
        if stage == 0:

            @pl.when(is_passage if name == FEW_ALL else is_query)
            def _():
                src = r.few_out.at[EARLY] if name == FEW_ALL else my_piece(name)
                remote(src, my_piece(name), send, recv, (1 - grp, bat)).start()

            return

        @pl.when(goes_to(name))
        def _():
            if stage == 1:
                piece = my_piece(name)
                for ahead in range(1, depth):
                    to = (lax.rem(lay + ahead, depth) * across + col) * 2 + core
                    remote(piece, piece, send, recv, (grp, to)).start()
            elif stage == 2:
                piece = buf.at[core, col]
                for ahead in range(1, across):
                    to = (lay * across + lax.rem(col + ahead, across)) * 2 + core
                    remote(piece, piece, send, recv, (grp, to)).start()
            else:
                piece = buf.at[core]
                remote(piece, piece, send, recv, (grp, sibling)).start()

    def size_waits(name, stage, side):
        buf = gathered[name]
        sem = sems(name, stage)[side]
        if stage == 0:
            if name == FEW_ALL or name in TO_PASSAGE:

                @pl.when(is_passage if (name == FEW_ALL) == (side == 0) else is_query)
                def _():
                    hold(sem, my_piece(name))

            return

        @pl.when(goes_to(name))
        def _():
            if stage == 1:
                hold(sem, buf.at[core, col, pl.ds(0, depth - 1)])
            elif stage == 2:
                hold(sem, buf.at[core, pl.ds(0, across - 1)])
            else:
                hold(sem, buf.at[core])

    def come(name, stage):
        size_waits(name, stage, 1)

    def sent(name):
        for stage in range(4):
            size_waits(name, stage, 0)

    def step_on(name, stage):
        come(name, stage - 1)
        go(name, stage)

    def few_go():
        @pl.when(is_passage)
        def _():
            dst = r.few_all.at[LATE, core, col, lay]

            def push(step, carry):
                other = lax.rem(bat + 2 * step, members)
                remote(r.few_out.at[LATE], dst, r.f_send.at[0], r.f_recv.at[0], (0, other)).start()
                return carry

            lax.fori_loop(0, members // 2, push, 0)

    def few_turn():
        whole = r.few_all.at[LATE, core]
        hold(r.f_recv.at[0], whole)
        remote(whole, whole, r.f_send.at[1], r.f_recv.at[1], (grp, sibling)).start()

    def few_come():
        @pl.when(is_query)
        def _():
            hold(r.f_recv.at[1], r.few_all.at[LATE, core])

        come(LAST_ALL, 3)

    def few_sent():
        @pl.when(is_query)
        def _():
            hold(r.f_send.at[1], r.few_all.at[LATE, core])

        @pl.when(is_passage)
        def _():
            hold(r.f_send.at[0], r.few_all.at[LATE, core])

    def share_rows(member):
        return pl.ds(pl.multiple_of(member * share, share), share)

    def spread(src, dst, at, to_grp, first_step, end_step=members):
        send, recv = r.a_send.at[at], r.a_recv.at[at]

        def push(step, carry):
            other = lax.rem(bat + step, members)
            remote(src(share_rows(other)), dst(my_slot), send, recv, (to_grp, other)).start()
            return carry

        lax.fori_loop(first_step, end_step, push, 0)

    def spread_t(first_step, end_step):
        spread(lambda rows: r.t_side.at[:, rows], lambda slot: r.side_got.at[slot, pl.ds(0, 3)], 0, 0, first_step, end_step)

    def sum_peer(step):
        if step == 0:
            return (1 - grp, bat)
        if step in (1, 2):
            other = lay + 1 - 2 * lax.rem(lay, 2) if step == 1 else lax.rem(lay + 2, depth)
            return (grp, (other * across + col) * 2 + core)
        if step == 3:
            return (grp, (lay * across + 1 - col) * 2 + core)
        return (grp, sibling)

    def sum_go(step):
        remote(
            r.sum_out.at[step], r.sum_in.at[step], r.v_send.at[step], r.v_recv.at[step], sum_peer(step)
        ).start()

    def sum_come(step):
        hold(r.v_recv.at[step], r.sum_in.at[step])
        r.sum_out[step + 1] = r.sum_out[step] + r.sum_in[step]

    load(TOKENS).wait()
    for at in (W_VALUE, W_OUT, W_IN, W_BACK):
        load(at).start()
    for copy in vector_loads:
        copy.wait()
    for at in range(len(vectors)):
        r.rows_v[at : at + 1, :] = r.vectors_v[at].reshape(1, width)
    r.b_in_v[...] = r.b_in_1d[...].reshape(1, hidden)
    place_col, _ = listed(iota((cand, 1), 0))
    _, seg_col = listed(iota((lanes, 1), 0) & (cand - 1))
    tokens_v = r.tokens_v
    pick = low(jnp.where(iota((cand, rows), 1) == place_col, 1.0, 0.0))
    r.left[2 * lanes : 2 * lanes + cand, :] = pick
    r.left[2 * lanes + cand : 2 * lanes + 2 * cand, :] = pick
    x_cls = nn(pick, tokens_v[...])
    x_low = low(x_cls)
    keep(X_ALL, x_low)
    pl.semaphore_wait(barrier, 2 * members - 1)
    go(X_ALL, 1)
    load(W_QUERY).wait()
    load(W_KEY).wait()
    q_cls = by_head(low(nn(x_low, r.w_query_v[...]) + vec(B_QUERY)))
    key_query = low(nt(q_cls, r.w_key_v[...]) * HD ** (-0.5))
    r.right[lanes : 2 * lanes, :] = key_query
    scores = nt(key_query, tokens_v[...])
    scores = jnp.where(seg_col == key_segment, scores, -1e30)
    raised = jnp.exp(scores - jnp.max(scores, axis=-1, keepdims=True))
    prob = raised / jnp.sum(raised, axis=-1, keepdims=True)
    r.prob[...] = prob
    r.left[0:lanes, :] = low(prob)
    value_sum = nn(r.left[0:lanes, :], tokens_v[...])
    @pl.when(is_query)
    def _():
        for v in range(lanes // 128):
            r.u_side[v] = low(value_sum[128 * v : 128 * v + 128].T)
        spread(lambda rows: r.u_side.at[pl.ds(0, 2), rows], lambda slot: r.side_got.at[slot, pl.ds(0, 2)], 4, 1, 0)

    @pl.when(is_passage)
    def _():
        r.u_few[...] = few_rows(value_sum)
        spread(lambda rows: r.u_few.at[rows], lambda slot: r.side_got.at[slot, 3], 3, 1, 1)

    load(W_VALUE).wait()
    load(W_OUT).wait()
    mixed = low(pick_heads(nn(low(value_sum), r.w_value_v[...])) + vec(B_VALUE))
    keep(MIXED_ALL, mixed)
    unit_one, rate_one = unit_rows(x_cls + nn(mixed, r.w_out_v[...]) + vec(B_OUT))
    normed = unit_one * vec(GAIN_ATTN) + vec(SHIFT_ATTN)
    normed_low = low(normed)
    keep(NORMED_ALL, normed_low)
    r.unit_one[...] = unit_one
    r.rate_one[...] = rate_one
    load(W_IN).wait()
    load(W_BACK).wait()
    active, slope = gelu_both(nn(normed_low, r.w_in_v[...]) + r.b_in_v[...])
    r.slope[...] = slope
    unit_two, rate_two = unit_rows(normed + nn(low(active), r.w_back_v[...]) + vec(B_BACK))
    r.unit_two[...] = unit_two
    r.rate_two[...] = rate_two
    cls = low(unit_two * vec(GAIN_FFN) + vec(SHIFT_FFN))
    r.cls[...] = cls


    per_core = (groups - 1) * members // 2
    lanes_n = 2 * per_core * 8

    @pl.when(is_passage)
    def _():
        r.pas_out[...] = pack_eight(cls[0:8])

        def push(k, carry):
            at = (grp - 1) * (members // 2) + lax.div(bat, 2)
            remote(
                r.pas_out, r.pas_in.at[core, at], r.b_send.at[0], r.b_recv.at[0], (0, 2 * k + core)
            ).start()
            return carry

        lax.fori_loop(0, members // 2, push, 0)

    for name in (NORMED_ALL, MIXED_ALL):
        go(name, 0)
    go(FEW_ALL, 0)


    def rank_rows():
        hold(r.b_recv.at[0], r.pas_in.at[core])
        mine = r.pas_in.at[core]
        remote(mine, mine, r.b_send.at[1], r.b_recv.at[1], (grp, sibling)).start()
        pos_col = jnp.zeros((cand, 1), jnp.int32)
        row = iota((cand, 1), 0)
        for s in range(cand):
            pos_col = jnp.where(row == s, r.positives[bat * cand + s], pos_col)
        spot = iota((1, lanes_n), 1)
        within = spot & 7
        owner = spot >> 3
        owner_core = lax.div(owner, per_core)
        owner = owner - owner_core * per_core
        owner_grp = lax.div(owner, members // 2)
        owner = (owner - owner_grp * (members // 2)) * 2 + owner_core + owner_grp * members
        real = within < PAS_DEV
        number = jnp.where(real, owner * PAS_DEV + within, -1)
        hold(r.b_recv.at[1], r.pas_in.at[1 - core])
        passages = low(unpack_eight(r.pas_in[...].reshape(2 * per_core, PART, half)))
        queries = r.cls[...]
        ranks = jnp.where(real, nt(queries, passages) * score_scale, -1e30)
        grown = jnp.exp(ranks - jnp.max(ranks, axis=-1, keepdims=True))
        soft = grown / jnp.sum(grown, axis=-1, keepdims=True)
        rank_grad = low(jnp.where(real, soft - jnp.where(number == pos_col, 1.0, 0.0), 0.0))
        r.y_grad[...] = nn(rank_grad, passages) * score_scale
        terms = (tn(rank_grad, queries) * score_scale).reshape(2 * per_core, 8, width)
        r.pas_part[...] = low(
            jnp.concatenate([terms[:, :, :half], terms[:, :, half:]], axis=1)
        ).reshape(2, per_core, PART, half)
        remote(
            r.pas_part.at[1 - core], r.pas_twin, r.b_send.at[2], r.b_recv.at[2], (grp, sibling)
        ).start()
        hold(r.b_recv.at[2], r.pas_twin)
        r.pas_sum[...] = low(wide(r.pas_part[core]) + wide(r.pas_twin[...]))

        def push(at, carry):
            to = (1 + lax.div(at, members // 2), 2 * lax.rem(at, members // 2) + core)
            remote(
                r.pas_sum.at[at], r.pas_got.at[lax.div(bat, 2)], r.b_send.at[3], r.b_recv.at[3], to
            ).start()
            return carry

        lax.fori_loop(0, per_core, push, 0)

    def passage_rows():
        hold(r.b_recv.at[3], r.pas_got)
        total = jnp.sum(wide(r.pas_got[...]), axis=0)
        r.y_grad[0:8, :] = jnp.concatenate([total[0:8], total[8:16]], axis=1)
        r.y_grad[8:cand, :] = jnp.zeros((cand - 8, width), jnp.float32)

    def backward_rows():
        y_grad = r.y_grad[...]
        unit = r.unit_two[...]
        gain_sum = jnp.sum(y_grad * unit, axis=0, keepdims=True)
        shift_sum = jnp.sum(y_grad, axis=0, keepdims=True)
        two_grad = norm_back(y_grad, unit, r.rate_two[...], vec(GAIN_FFN))
        branch = low(two_grad)
        keep(BRANCH_ALL, branch)
        go(BRANCH_ALL, 0)

        @pl.when(is_query)
        def _():
            go(BRANCH_ALL, 1)

        pre_grad = low(nt(branch, r.w_back_v[...]) * r.slope[...])
        pre_sum = jnp.sum(wide(pre_grad), axis=0, keepdims=True)
        normed_grad = two_grad + nt(pre_grad, r.w_in_v[...])
        unit = r.unit_one[...]
        gain_one = jnp.sum(normed_grad * unit, axis=0, keepdims=True)
        shift_one = jnp.sum(normed_grad, axis=0, keepdims=True)
        one_grad = norm_back(normed_grad, unit, r.rate_one[...], vec(GAIN_ATTN))
        attn = low(one_grad)
        keep(ATTN_ALL, attn)
        go(ATTN_ALL, 0)
        go(LAST_ALL, 1)
        mixed_low = low(nt(attn, r.w_out_v[...]))
        mixed_grad = by_head(mixed_low)
        value_mix = low(nt(mixed_grad, r.w_value_v[...]))
        r.right[0:lanes, :] = value_mix
        prob_grad = nt(value_mix, tokens_v[...])
        prob = r.prob[...]
        score_grad = low(prob * (prob_grad - jnp.sum(prob * prob_grad, axis=-1, keepdims=True)))
        r.left[lanes : 2 * lanes, :] = score_grad
        token_sum = nn(score_grad, tokens_v[...])
        query_grad = low(pick_heads(nn(low(token_sum), r.w_key_v[...])) * HD ** (-0.5))
        keep(QUERY_ALL, query_grad)
        go(QUERY_ALL, 1)
        few_go()
        r.t_sum[...] = token_sum
        col_sums = [jnp.sum(wide(v), axis=0, keepdims=True) for v in (query_grad, mixed_low, attn, branch)]
        r.sum_out[0] = jnp.concatenate(
            [gain_sum, shift_sum, gain_one, shift_one]
            + col_sums
            + [pre_sum[:, width * j : width * (j + 1)] for j in range(hidden // width)]
            + [jnp.zeros((8 - hidden // width, width), jnp.float32)],
            axis=0,
        )
        sum_go(0)

        @pl.when(is_query)
        def _():
            remote(r.u_side.at[2], r.u_twin, r.a_send.at[2], r.a_recv.at[2], (1, bat)).start()

        row_grad = one_grad + nt(query_grad, r.w_query_v[...])
        row_high = low(row_grad)
        r.right[2 * lanes : 2 * lanes + cand, :] = row_high
        r.right[2 * lanes + cand : 2 * lanes + 2 * cand, :] = low(row_grad - wide(row_high))
        pltpu.make_async_copy(r.left, r.left_out, r.store_sem.at[1]).start()
        pltpu.make_async_copy(r.right, r.right_out, r.store_sem.at[2]).start()

    tile = 256
    tiles = rows // tile
    first_half = iota((1, 128), 1) < HD
    half_on = low(jnp.where(first_half, 1.0, 0.0))
    half_off = low(jnp.where(first_half, 0.0, 1.0))
    one_lanes = jnp.full((tile, 128), 1.0, jnp.bfloat16)

    def attend_tile(i):
        at = pl.multiple_of(i * tile, tile)
        tok = tokens_v[pl.ds(at, tile), :]
        query = low(nn(tok, r.w_query_v[...]) + vec(B_QUERY)) * jnp.bfloat16(HD ** (-0.5))
        key = low(nn(tok, r.w_key_v[...]))
        value = low(nn(tok, r.w_value_v[...]) + vec(B_VALUE))
        token_col = iota((tile, 1), 0) + at
        bucket = jnp.where(i < BLK // tile, first, second)
        segment, _ = segment_of(token_col, bucket)
        unseen = jnp.where(segment == r.key_seg[i], 0.0, -1e30)
        outs = []
        for pair in range(H // 2):
            span = slice(128 * pair, 128 * pair + 128)
            q_pair, k_pair, v_pair = query[:, span], key[:, span], value[:, span]
            value_one = jnp.concatenate([v_pair, one_lanes], axis=1)
            parts = []
            for side in (half_on, half_off):
                s = nt(q_pair * side, k_pair) + unseen
                e = jnp.exp(s - jnp.max(s, axis=-1, keepdims=True))
                both = nn(low(e), value_one)
                parts.append(both[:, :128] / both[:, 128:])
            outs.append(low(jnp.where(first_half, parts[0], parts[1])))
        mixed_tile = jnp.concatenate(outs, axis=1)
        unit_tile, _ = unit_rows(wide(tok) + nn(mixed_tile, r.w_out_v[...]) + vec(B_OUT))
        r.normed_v[...] = unit_tile * vec(GAIN_ATTN) + vec(SHIFT_ATTN)

    def feed_tile(i):
        at = pl.multiple_of(i * tile, tile)
        normed_tile = r.normed_v[...]
        low_tile = low(normed_tile)
        total = normed_tile + vec(B_BACK)
        span = hidden // 4
        pre = nn(low_tile, r.w_in_v[:, 0:span]) + r.b_in_v[:, 0:span]
        for j in range(4):
            ahead = slice((j + 1) * span, (j + 2) * span)
            if j < 3:
                later = nn(low_tile, r.w_in_v[:, ahead]) + r.b_in_v[:, ahead]
            total = total + nn(low(gelu(pre)), r.w_back_v[j * span : (j + 1) * span, :])
            pre = later
        unit_tile, _ = unit_rows(total)
        r.enc_v[pl.ds(at, tile), :] = low(unit_tile * vec(GAIN_FFN) + vec(SHIFT_FFN))
        spot = pl.ds(at, tile)
        pltpu.make_async_copy(r.enc_v.at[spot], r.encoded.at[spot], r.store_sem.at[0]).start()

    def sum_step(step):
        def act():
            sum_come(step - 1)
            sum_go(step)

        return act

    def stage_step(name, stage):
        return lambda: step_on(name, stage)

    def twin_spread():
        hold(r.a_recv.at[2], r.u_twin)
        spread(lambda rows: r.u_twin.at[rows], lambda slot: r.side_got.at[slot, 2], 5, 1, 1)

    def many_spread():
        for v in range(lanes // 128):
            r.t_side[v] = low(r.t_sum[128 * v : 128 * v + 128].T)
        spread_t(1, members)

    def few_push():
        r.t_few[...] = few_rows(r.t_sum[...])
        remote(r.t_few, r.t_twin, r.a_send.at[1], r.a_recv.at[1], (0, bat)).start()

    def few_spread():
        hold(r.a_recv.at[1], r.t_twin)
        spread(lambda rows: r.t_twin.at[rows], lambda slot: r.side_got.at[slot, 3], 6, 0, 1)

    QUERY_MOVES = {
        0: [stage_step(NORMED_ALL, 2), stage_step(X_ALL, 3)],
        2: [stage_step(BRANCH_ALL, 2), stage_step(NORMED_ALL, 3)],
        3: [sum_step(1), stage_step(FEW_ALL, 1), stage_step(QUERY_ALL, 2)],
        4: [sum_step(2), many_spread, stage_step(BRANCH_ALL, 3)],
        5: [few_turn, stage_step(FEW_ALL, 2)],
        6: [few_spread, sum_step(3)],
        7: [sum_step(4), stage_step(FEW_ALL, 3)],
        8: [stage_step(QUERY_ALL, 3)],
    }
    PASSAGE_MOVES = {
        1: [stage_step(NORMED_ALL, 1)],
        2: [sum_step(1), few_push, lambda: go(FEW_ALL, 1), stage_step(NORMED_ALL, 2)],
        3: [stage_step(ATTN_ALL, 1), stage_step(BRANCH_ALL, 2)],
        4: [sum_step(2), stage_step(MIXED_ALL, 1), stage_step(LAST_ALL, 2), stage_step(NORMED_ALL, 3)],
        5: [twin_spread, stage_step(FEW_ALL, 2), stage_step(BRANCH_ALL, 3)],
        6: [stage_step(ATTN_ALL, 2), stage_step(LAST_ALL, 3)],
        7: [sum_step(3), stage_step(MIXED_ALL, 2), stage_step(FEW_ALL, 3)],
        8: [],
    }

    def moves(i, odd):
        for table, where in ((QUERY_MOVES, is_query), (PASSAGE_MOVES, is_passage)):
            for point, acts in table.items():
                if point // 2 < tiles and point % 2 == odd:

                    @pl.when(jnp.logical_and(i == point // 2, where))
                    def _():
                        for act in acts:
                            act()

    def turn(i, carry):
        attend_tile(i)

        @pl.when(jnp.logical_and(i == 0, is_query))
        def _():
            rank_rows()
            go(NORMED_ALL, 1)
            step_on(X_ALL, 2)

        @pl.when(jnp.logical_and(i == 1, is_passage))
        def _():
            passage_rows()
            step_on(BRANCH_ALL, 1)

        @pl.when(i == jnp.where(is_query, 0, 1))
        def _():
            backward_rows()

        moves(i, 0)
        feed_tile(i)
        moves(i, 1)
        return carry

    lax.fori_loop(0, tiles, turn, 0)

    for table, where in ((QUERY_MOVES, is_query), (PASSAGE_MOVES, is_passage)):

        @pl.when(where)
        def _():
            for act in table[2 * tiles]:
                act()


    def flatten(name, dst):
        rows_q = gathered[name][...].reshape(slots, 2 * cand, half)
        dst[0:query_rows, 0:half] = rows_q[:, 0:cand].reshape(query_rows, half)
        dst[0:query_rows, half:width] = rows_q[:, cand : 2 * cand].reshape(query_rows, half)
        when, at = divmod((TO_QUERY if name in TO_QUERY else TO_PASSAGE).index(name), 2)
        rows_p = r.few_all[when, :, :, :, PART * at : PART * at + PART].reshape(slots, PART, half)
        dst[query_rows:all_rows, :] = low(unpack_eight(rows_p))

    win = 256
    at48 = bat * share
    base48 = jnp.minimum(lax.div(at48, 128) * 128, width - win)
    off48 = pl.multiple_of(at48 - base48, 8)
    win48 = pl.ds(pl.multiple_of(base48, 128), win)
    share_in = hidden // members
    at192 = bat * share_in
    base192 = jnp.minimum(lax.div(at192, 128) * 128, hidden - win)
    off192 = pl.multiple_of(at192 - base192, 8)
    win192 = pl.ds(pl.multiple_of(base192, 128), win)
    mine48 = pl.ds(off48, share)
    side = hidden // 2
    own_side = pl.multiple_of(grp * side, 128)
    other_side = pl.multiple_of((1 - grp) * side, 128)

    def swap(at, src, dst):
        remote(src, dst, r.s_send.at[at], r.s_recv.at[at], (1 - grp, bat)).start()

    come(FEW_ALL, 3)
    few_come()
    come(NORMED_ALL, 3)
    flatten(NORMED_ALL, r.flat_a)
    come(BRANCH_ALL, 3)
    flatten(BRANCH_ALL, r.flat_b)
    step = side // 2

    def slope_cols(j, carry):
        span = pl.ds(pl.multiple_of(own_side + j * step, 128), step)
        slope_j = gelu_slope(nn(r.flat_a[...], r.w_in_v[:, span]) + r.b_in_v[:, span])
        pre_j = low(nt(r.flat_b[...], r.w_back_v[span, :]) * slope_j)
        here = pl.ds(pl.multiple_of(j * step, 128), step)
        r.stage[:, here] = tn(r.flat_a[:, win48], pre_j)
        return carry

    lax.fori_loop(0, 2, slope_cols, 0)
    piece = low(r.stage[mine48, :])
    r.swap_out0[...] = piece
    swap(0, r.swap_out0, r.swap_in0)
    r.g_in[:, pl.ds(own_side, side)] = wide(piece)
    def back_share():
        active_win = low(gelu(nn(r.flat_a[...], r.w_in_v[:, win192]) + r.b_in_v[:, win192]))
        r.stage[:, 0:width] = tn(active_win, r.flat_b[...])
        r.g_back[...] = r.stage[pl.ds(off192, share_in), 0:width]

    @pl.when(is_passage)
    def _():
        sum_step(4)()
        step_on(ATTN_ALL, 3)
        step_on(MIXED_ALL, 3)
        back_share()


    def one_share(left, right):
        r.stage[:, 0:width] = tn(left[:, win48], right[...])
        r.swap_out1[0] = low(r.stage[mine48, 0:width])
        swap(1, r.swap_out1.at[0], r.swap_in1.at[0])

    @pl.when(is_query)
    def _():
        come(X_ALL, 3)
        flatten(X_ALL, r.flat_c)
        come(QUERY_ALL, 3)
        flatten(QUERY_ALL, r.flat_d)
        one_share(r.flat_c, r.flat_d)
        r.factor[...] = (nn(r.flat_c[...], r.w_query_v[...]) + vec(B_QUERY)) * HD ** (-0.5)
        r.side_got[my_slot, 0:3] = r.t_side[:, share_rows(bat)]
        r.side_got[my_slot, 3] = r.t_twin[share_rows(bat)]
        hold(r.a_recv.at[0], r.side_got.at[pl.ds(0, members - 1), pl.ds(0, 3)])
        hold(r.a_recv.at[6], r.side_got.at[pl.ds(0, members - 1), 3])

    @pl.when(is_passage)
    def _():
        come(MIXED_ALL, 3)
        flatten(MIXED_ALL, r.flat_c)
        come(ATTN_ALL, 3)
        flatten(ATTN_ALL, r.flat_d)
        one_share(r.flat_c, r.flat_d)
        r.factor[...] = nt(r.flat_d[...], r.w_out_v[...])
        r.side_got[my_slot, 2] = r.u_twin[share_rows(bat)]
        r.side_got[my_slot, 3] = r.u_few[share_rows(bat)]
        hold(r.a_recv.at[4], r.side_got.at[:, pl.ds(0, 2)])
        hold(r.a_recv.at[5], r.side_got.at[pl.ds(0, members - 1), 2])
        hold(r.a_recv.at[3], r.side_got.at[pl.ds(0, members - 1), 3])

    head_4 = iota((1, HEADS_VREG, 1, HEADS_VREG * HD), 1)
    lane_4 = iota((1, HEADS_VREG, 1, HEADS_VREG * HD), 3) >> 6
    head_16 = iota((1, 16, 1, HEADS_VREG * HD), 1)
    lane_16 = iota((1, 16, 1, HEADS_VREG * HD), 3) >> 6
    few = jnp.concatenate([r.side_got[m, 3] for m in range(slots)], axis=1)
    for v in range(H // HEADS_VREG):
        span = slice(256 * v, 256 * v + 256)
        left = jnp.concatenate([r.side_got[m, v] for m in range(slots)], axis=1)
        full = r.factor[0:query_rows, span].reshape(slots, 1, cand, 256)
        right = low(jnp.where(head_4 == lane_4, full, 0.0)).reshape(slots * 128, 256)
        total = nn(left, right)
        full = r.factor[query_rows:all_rows, span].reshape(slots, 1, 8, 256)
        right = low(jnp.where(head_16 == lane_16 + HEADS_VREG * v, full, 0.0)).reshape(slots * 128, 256)
        r.swap_out1[1, :, span] = low(total + nn(few, right))
    swap(2, r.swap_out1.at[1], r.swap_in1.at[1])

    @pl.when(is_query)
    def _():
        back_share()


    @pl.when(is_query)
    def _():
        r.g_query[...] = wide(r.swap_out1[0])
        r.g_key[...] = wide(r.swap_out1[1])

    @pl.when(is_passage)
    def _():
        r.g_out[...] = wide(r.swap_out1[0])
        r.g_value[...] = wide(r.swap_out1[1])

    sum_come(4)
    mine = pltpu.roll(r.sum_out[5, 0:8], lax.rem(width - at48, width), 1)
    shares = (
        r.g_gain_ffn,
        r.g_shift_ffn,
        r.g_gain_attn,
        r.g_shift_attn,
        r.gb_query,
        r.gb_value,
        r.gb_out,
        r.gb_back,
    )
    for at, ref in enumerate(shares):
        ref[...] = mine[at : at + 1, 0:share].reshape(share)
    line = r.sum_out[5, pl.ds(8 + lax.div(at192, width), 1), :]
    line = pltpu.roll(
        jnp.broadcast_to(line, (8, width)), lax.rem(width - lax.rem(at192, width), width), 1
    )
    r.gb_in[...] = line[0:1, 0:share_in].reshape(share_in)

    hold(r.s_recv.at[0], r.swap_in0)
    r.g_in[:, pl.ds(other_side, side)] = wide(r.swap_in0[...])
    hold(r.s_recv.at[1], r.swap_in1.at[0])
    hold(r.s_recv.at[2], r.swap_in1.at[1])

    @pl.when(is_query)
    def _():
        r.g_out[...] = wide(r.swap_in1[0])
        r.g_value[...] = wide(r.swap_in1[1])

    @pl.when(is_passage)
    def _():
        r.g_query[...] = wide(r.swap_in1[0])
        r.g_key[...] = wide(r.swap_in1[1])

    hold(r.store_sem.at[0], r.enc_v)
    hold(r.store_sem.at[1], r.left)
    hold(r.store_sem.at[2], r.right)
    for name in range(len(gathered)):
        sent(name)
    few_sent()
    for at in range(5):
        hold(r.v_send.at[at], r.sum_out.at[at])
    hold(r.s_send.at[0], r.swap_out0)
    hold(r.s_send.at[1], r.swap_out1.at[0])
    hold(r.s_send.at[2], r.swap_out1.at[1])

    @pl.when(is_query)
    def _():
        hold(r.a_send.at[0], r.side_got.at[pl.ds(0, members - 1), pl.ds(0, 3)])
        hold(r.a_send.at[6], r.side_got.at[pl.ds(0, members - 1), 3])
        hold(r.a_send.at[2], r.u_twin)
        hold(r.a_send.at[4], r.side_got.at[:, pl.ds(0, 2)])
        hold(r.b_send.at[1], r.pas_in.at[core])
        hold(r.b_send.at[2], r.pas_twin)
        hold(r.b_send.at[3], r.pas_sum)

    @pl.when(is_passage)
    def _():
        hold(r.a_send.at[1], r.t_few)
        hold(r.a_send.at[3], r.side_got.at[pl.ds(0, members - 1), 3])
        hold(r.a_send.at[5], r.side_got.at[pl.ds(0, members - 1), 2])
        hold(r.b_send.at[0], r.pas_got)


def result_kernel(count, *refs):
    ins, outs = refs[: count + 1], refs[count + 1 : 2 * count + 1]
    held, (tile_out, load_sem, store_sem, grad_sem) = refs[2 * count + 1 : -4], refs[-4:]
    loads = [pltpu.make_async_copy(src, dst, load_sem.at[at]) for at, (src, dst) in enumerate(zip(ins, held))]
    for at in (1, 2, 0) + tuple(range(3, count + 1)):
        loads[at].start()
    places = (0,) + tuple(range(2, count))
    stores = [
        pltpu.make_async_copy(held[at + 1 if at else 0], outs[at], store_sem.at[at]) for at in places
    ]
    loads[1].wait()
    loads[2].wait()
    tile = tile_out.shape[0] // 4
    grads = []
    for i in range(4):
        spot = slice(i * tile, (i + 1) * tile)
        tile_out[spot, :] = tn(held[1][:, spot], held[2][...])
        grads.append(pltpu.make_async_copy(tile_out.at[spot], outs[1].at[spot], grad_sem.at[i]))
        grads[-1].start()
        if i == 0:
            for at, store in zip(places, stores):
                loads[at + 1 if at else 0].wait()
                store.start()
    for copy in grads + stores:
        copy.wait()


def make_shards(groups, members):
    def shards(*args):
        tokens = args[0]
        rows, width = tokens.shape
        hidden = Ins(*args).w_in.shape[1]
        share, share_in = width // members, hidden // members
        cand = rows // QLEN
        lanes = H * cand
        all_rows = members * (cand + 8)
        per_core = (groups - 1) * members // 2
        across = members // 8
        half = width // 2
        f32, bf16 = jnp.float32, jnp.bfloat16
        out_shapes = Outs(
            encoded=((rows, width), bf16),
            left_out=((2 * lanes + 2 * cand, rows), bf16),
            right_out=((2 * lanes + 2 * cand, width), bf16),
            g_query=((share, width), f32),
            gb_query=((share,), f32),
            g_key=((share, width), f32),
            g_value=((share, width), f32),
            gb_value=((share,), f32),
            g_out=((share, width), f32),
            gb_out=((share,), f32),
            g_gain_attn=((share,), f32),
            g_shift_attn=((share,), f32),
            g_in=((share, hidden), f32),
            gb_in=((share_in,), f32),
            g_back=((share_in, width), f32),
            gb_back=((share,), f32),
            g_gain_ffn=((share,), f32),
            g_shift_ffn=((share,), f32),
        )
        out_shape = tuple(jax.ShapeDtypeStruct(*pair) for pair in out_shapes)
        dma = pltpu.SemaphoreType.DMA
        gathered = pltpu.VMEM((2, across, 4, 2 * cand, half), bf16)
        scratch = Scratch(
            tokens_v=pltpu.VMEM((rows, width), bf16),
            w_query_v=pltpu.VMEM((width, width), bf16),
            w_key_v=pltpu.VMEM((width, width), bf16),
            w_value_v=pltpu.VMEM((width, width), bf16),
            w_out_v=pltpu.VMEM((width, width), bf16),
            w_in_v=pltpu.VMEM((width, hidden), bf16),
            w_back_v=pltpu.VMEM((hidden, width), bf16),
            vectors_v=pltpu.VMEM((8, width), f32),
            b_in_1d=pltpu.VMEM((hidden,), f32),
            vector_sem=dma((9,)),
            rows_v=pltpu.VMEM((8, width), f32),
            t_sum=pltpu.VMEM((lanes, width), f32),
            b_in_v=pltpu.VMEM((1, hidden), f32),
            key_seg=pltpu.VMEM((rows // 256, 1, 256), jnp.int32),
            left=pltpu.VMEM((2 * lanes + 2 * cand, rows), bf16),
            right=pltpu.VMEM((2 * lanes + 2 * cand, width), bf16),
            prob=pltpu.VMEM((lanes, rows), f32),
            slope=pltpu.VMEM((cand, hidden), f32),
            unit_one=pltpu.VMEM((cand, width), f32),
            rate_one=pltpu.VMEM((cand, 1), f32),
            unit_two=pltpu.VMEM((cand, width), f32),
            rate_two=pltpu.VMEM((cand, 1), f32),
            cls=pltpu.VMEM((cand, width), bf16),
            y_grad=pltpu.VMEM((cand, width), f32),
            x_all=gathered,
            mixed_all=gathered,
            normed_all=gathered,
            branch_all=gathered,
            attn_all=gathered,
            query_all=gathered,
            few_all=pltpu.VMEM((2, 2, across, 4, 2 * PART, half), bf16),
            few_out=pltpu.VMEM((2, 2 * PART, half), bf16),
            t_side=pltpu.VMEM((lanes // 128, width, 128), bf16),
            u_side=pltpu.VMEM((lanes // 128, width, 128), bf16),
            u_twin=pltpu.VMEM((width, 128), bf16),
            t_few=pltpu.VMEM((width, 128), bf16),
            u_few=pltpu.VMEM((width, 128), bf16),
            side_got=pltpu.VMEM((members, lanes // 128 + 1, share, 128), bf16),
            t_twin=pltpu.VMEM((width, 128), bf16),
            sum_out=pltpu.VMEM((6, 16, width), f32),
            sum_in=pltpu.VMEM((5, 16, width), f32),
            pas_out=pltpu.VMEM((PART, half), bf16),
            pas_in=pltpu.VMEM((2, per_core, PART, half), bf16),
            pas_part=pltpu.VMEM((2, per_core, PART, half), bf16),
            pas_twin=pltpu.VMEM((per_core, PART, half), bf16),
            pas_sum=pltpu.VMEM((per_core, PART, half), bf16),
            pas_got=pltpu.VMEM((members // 2, PART, half), bf16),
            normed_v=pltpu.VMEM((256, width), f32),
            enc_v=pltpu.VMEM((rows, width), bf16),
            flat_a=pltpu.VMEM((all_rows, width), bf16),
            flat_b=pltpu.VMEM((all_rows, width), bf16),
            flat_c=pltpu.VMEM((all_rows, width), bf16),
            flat_d=pltpu.VMEM((all_rows, width), bf16),
            factor=pltpu.VMEM((all_rows, width), f32),
            stage=pltpu.VMEM((256, hidden // 2), f32),
            swap_out0=pltpu.VMEM((share, hidden // 2), bf16),
            swap_in0=pltpu.VMEM((share, hidden // 2), bf16),
            swap_out1=pltpu.VMEM((2, share, width), bf16),
            swap_in1=pltpu.VMEM((2, share, width), bf16),
            load_sem=dma((7,)),
            store_sem=dma((3,)),
            g_send=dma((8, 4)),
            g_recv=dma((8, 4)),
            f_send=dma((2,)),
            f_recv=dma((2,)),
            v_send=dma((5,)),
            v_recv=dma((5,)),
            a_send=dma((7,)),
            a_recv=dma((7,)),
            b_send=dma((4,)),
            b_recv=dma((4,)),
            s_send=dma((3,)),
            s_recv=dma((3,)),
        )
        anywhere = pl.BlockSpec(memory_space=pl.ANY)
        vmem = pl.BlockSpec(memory_space=pltpu.VMEM)
        smem = pl.BlockSpec(memory_space=pltpu.SMEM)
        in_specs = [anywhere] * len(args)
        for at in range(1, 4):
            in_specs[at] = smem
        out_specs = (anywhere,) * 3 + (vmem,) * (len(out_shape) - 3)
        made = pl.pallas_call(
            functools.partial(main_kernel, (groups, members, rows, width, hidden)),
            out_shape=out_shape,
            in_specs=in_specs,
            out_specs=out_specs,
            scratch_shapes=list(scratch),
            name="layer",
            compiler_params=pltpu.CompilerParams(
                collective_id=0, has_side_effects=True, vmem_limit_bytes=60 * 1024 * 1024
            ),
        )(*args)
        results = (out_shape[0], jax.ShapeDtypeStruct((rows, width), f32)) + out_shape[3:]
        count = len(results)
        return pl.pallas_call(
            functools.partial(result_kernel, count),
            out_shape=results,
            in_specs=[anywhere] * (count + 1),
            out_specs=(anywhere,) * count,
            scratch_shapes=[pltpu.VMEM(shape.shape, shape.dtype) for shape in out_shape]
            + [pltpu.VMEM((rows, width), f32), dma((count + 1,)), dma((count,)), dma((4,))],
            name="results",
            compiler_params=pltpu.CompilerParams(vmem_limit_bytes=60 * 1024 * 1024),
        )(*made)

    return shards


def solution(mesh):
    in_specs = (
        P(("grp", "batch"), None),
        P(("grp", "batch")),
        P(("grp", "batch"), None),
        P(),
        P(),
        P(),
        P(),
        P(),
        P(),
        P(),
        P(),
        P(),
        P(),
        P(),
        P(),
        P(),
        P(),
        P(),
        P(),
    )
    out_specs = (
        P(("grp", "batch"), None),
        P(("grp", "batch"), None),
        P("batch", None),
        P("batch"),
        P("batch", None),
        P("batch", None),
        P("batch"),
        P("batch", None),
        P("batch"),
        P("batch"),
        P("batch"),
        P("batch", None),
        P("batch"),
        P("batch", None),
        P("batch"),
        P("batch"),
        P("batch"),
    )
    groups, members = mesh.shape["grp"], mesh.shape["batch"]
    fits = groups == 2 and members == 16
    shards = make_shards(groups, members) if fits else plain_shards
    return jax.shard_map(shards, mesh=mesh, in_specs=in_specs, out_specs=out_specs, check_vma=False)
```
